256 devices in a mesh: tm: 16 (over z, core), evec: 16 (over y, x).
Axes of the slice: x: 4, y: 4, z: 8, core: 2. Of those that a mesh axis runs over, the one named last changes fastest.
Arguments:
- sink_elemental: bfloat16 [2, 16, 8, 128, 128, 128], P(None, 'tm', None, 'evec'), may hold values from -6 to 6
- source_elemental: bfloat16 [2, 8, 128, 128, 128], P(None, None, None, 'evec', 'tm'), may hold values from -6 to 6
- perambulator: bfloat16 [2, 16, 128, 128], P(None, 'tm'), may hold values from -0.375 to 0.375
- diagram_time: int32 [1024], replicated, may hold values from 0 to 15
- diagram_perm: int32 [1024, 2], replicated, may hold values from 0 to 1
- diagram_ops: int32 [1024, 4], replicated, may hold values from 0 to 7
- diagram_sign: int32 [1024], replicated, may hold values from 0 to 1
Outputs:
- blocks: float32 [2, 16, 2, 8, 8], P(None, 'tm')
- correlator: float32 [2, 16], P(None, 'tm')
The draws below stay inside these ranges and needn't reach their ends.
All inputs are finite; a program needn't handle non-finite values.
Results may differ from the reference program's by a relative error of at most 0.0003.
Values may be sent and summed in bfloat16 or wider, within the bound.
A program may use at most 128 MiB of HBM per device.

```python
import math
import jax
import jax.numpy as jnp
import numpy as np
from jax import lax

NEV = 128
NS = 8
DIAG_T = 64
TIME = 16
NDIAG = 1024


def set_ends(array, key, smallest, top_value):
    shape = array.shape
    place = [jax.random.randint(jax.random.fold_in(key, axis), (), 0, shape[axis]) for axis in range(len(shape))]
    array = array.at[tuple(place)].set(smallest)
    longest = shape.index(max(shape))
    place[longest] = (place[longest] + 1) % shape[longest]
    return array.at[tuple(place)].set(top_value)


def steps_of(stream_key, dims, shards, smallest, high):
    gain, own = 1.0, jax.random.fold_in(stream_key, 6)
    for axis_at, shards_of in shards:
        draws = jnp.exp(jax.random.uniform(jax.random.fold_in(own, axis_at), (shards_of,), jnp.float32, smallest / len(shards), high / len(shards)))
        gain = gain * jnp.repeat(draws, dims[axis_at] // shards_of).reshape([-1 if axis == axis_at else 1 for axis in range(len(dims))])
    return gain


def rank_table(count, lean):
    weights = [(1 << 20) // math.isqrt(grade ** lean) + 1 for grade in range(1, count + 1)]
    spread = 1 + sum(weights) // (1 << 30)
    return np.cumsum(np.array([max(1, weight // spread) for weight in weights]))


def ranked_ids(rng, shape, count, skew):
    grid = rank_table(count, skew)
    lot = jax.random.randint(jax.random.fold_in(rng, 1), shape, 0, int(grid[count - 1]))
    grade = jnp.searchsorted(jnp.asarray(grid, jnp.int32), lot, side="right")
    return jax.random.permutation(jax.random.fold_in(rng, 2), count)[grade].astype(jnp.int32)


def centred(own_key, extent, deviation, reach, pieces=(), kind=jnp.bfloat16):
    drawn = deviation * jax.random.normal(own_key, extent, jnp.float32)
    if pieces:
        drawn = drawn * steps_of(own_key, extent, pieces, -0.22, 0.18)
    return jnp.clip(drawn, -reach, reach).astype(kind)


def setup_inputs(seed: int = 0) -> dict:
    keys = jax.random.split(jax.random.key(seed), 8)
    return {
        "sink_elemental": centred(keys[0], (2, TIME, NS, NEV, NEV, NEV), 1.0, 6.0, ((1, 16), (3, 16))),
        "source_elemental": centred(keys[1], (2, NS, NEV, NEV, NEV), 1.0, 6.0, ((3, 16), (4, 16))),
        "perambulator": centred(keys[2], (2, TIME, NEV, NEV), (2 * NEV) ** -0.5, 0.375, ((1, 16),)),
        "diagram_time": set_ends(ranked_ids(keys[3], (NDIAG,), TIME, 2), jax.random.fold_in(keys[3], 3), 0, TIME - 1).astype(jnp.int32),
        "diagram_perm": set_ends(jax.random.randint(keys[4], (NDIAG, 2), 0, 2), jax.random.fold_in(keys[4], 1), 0, 1).astype(jnp.int32),
        "diagram_ops": set_ends(jax.random.randint(keys[5], (NDIAG, 4), 0, NS), jax.random.fold_in(keys[5], 1), 0, NS - 1).astype(jnp.int32),
        "diagram_sign": set_ends(jax.random.randint(keys[6], (NDIAG,), 0, 2), jax.random.fold_in(keys[6], 1), 0, 1).astype(jnp.int32),
    }


def contract(pattern, former, latter):
    exact = lax.Precision.HIGHEST
    real_part = jnp.einsum(pattern, former[0], latter[0], precision=exact) - jnp.einsum(pattern, former[1], latter[1], precision=exact)
    imaginary_part = jnp.einsum(pattern, former[0], latter[1], precision=exact) + jnp.einsum(pattern, former[1], latter[0], precision=exact)
    return jnp.stack([real_part, imaginary_part])

def reference(sink_elemental, source_elemental, perambulator, diagram_time, diagram_perm, diagram_ops, diagram_sign):
    source = source_elemental.astype(jnp.float32)
    swapped = jnp.transpose(source, (0, 1, 4, 3, 2))

    def one_time(time_index):
        sink_now = lax.dynamic_index_in_dim(sink_elemental, time_index, 1, keepdims=False).astype(jnp.float32)
        perambulator_now = lax.dynamic_index_in_dim(perambulator, time_index, 1, keepdims=False).astype(jnp.float32)
        section_one = contract('sabc,ck->sabk', sink_now, perambulator_now)
        section_two = contract('sabk,bj->sajk', section_one, perambulator_now)
        hadron = contract('sajk,ai->sijk', section_two, perambulator_now)
        direct = contract('sijk,uijk->su', hadron, source)
        crossed = contract('sijk,uijk->su', hadron, swapped)
        return jnp.stack([direct, crossed], axis=1)
    stacked = lax.map(one_time, jnp.arange(TIME, dtype=jnp.int32))
    blocks = jnp.moveaxis(stacked, 0, 1) * NEV ** (-1.5)
    first_pick = blocks[:, diagram_time, diagram_perm[:, 0], diagram_ops[:, 0], diagram_ops[:, 1]]
    second_pick = blocks[:, diagram_time, diagram_perm[:, 1], diagram_ops[:, 2], diagram_ops[:, 3]]
    phase_sign = 1.0 - 2.0 * diagram_sign.astype(jnp.float32)
    real_part = (first_pick[0] * second_pick[0] - first_pick[1] * second_pick[1]) * phase_sign
    imaginary_part = (first_pick[0] * second_pick[1] + first_pick[1] * second_pick[0]) * phase_sign
    weighted = jnp.stack([real_part, imaginary_part], axis=1)
    correlator = jax.ops.segment_sum(weighted, diagram_time, num_segments=TIME).T / math.sqrt(DIAG_T)
    return (blocks, correlator)
```

```python
import functools
import math

import jax
import jax.numpy as jnp
from jax import lax
from jax.experimental import pallas as pl
from jax.experimental.pallas import tpu as pltpu
from jax.sharding import PartitionSpec as P

DIAG_T = 64
NEV = 128
NS = 8
BLOCK = 8
EV = 16
TM = 16
ZS = 8
ROWS = NS * BLOCK
TOP = 32767.0
MESH = pl.DeviceIdType.MESH
F32 = jnp.float32
BF16 = jnp.bfloat16
NT = (((1,), (1,)), ((), ()))
NN = (((1,), (0,)), ((), ()))
FAR_FIRST = (10, 9, 11, 6, 14, 2, 8, 5, 7, 13, 15, 1, 3, 4, 12)


def split_parts(value):
    high = value.astype(BF16)
    return high, (value - high.astype(F32)).astype(BF16)


def iota(shape, axis):
    return lax.broadcasted_iota(jnp.int32, shape, axis)


def kernel(
    sink_ref,
    source_ref,
    peram_ref,
    time_ref,
    perm_ref,
    ops_ref,
    sign_ref,
    blocks_ref,
    corr_ref,
    sink_buf,
    send,
    recv,
    gathered,
    rmat,
    stage,
    tmat,
    total,
    scale_own,
    scale_recv,
    scale_wide,
    left_mat,
    right_mat,
    source_mat,
    counts,
    part_own,
    part_recv,
    sink_sem,
    send_sem,
    recv_sem,
    own_sem,
    scale_sem,
    part_sem,
    ring_sem,
    pair_sem,
    slot_sem,
):
    tm = lax.axis_index("tm")
    ev = lax.axis_index("evec")
    row, column = ev // 4, lax.rem(ev, 4)
    depth, core = tm // 2, lax.rem(tm, 2)

    def peer(step):
        return lax.rem(row + step // 4, 4) * 4 + lax.rem(column + step % 4, 4)

    def slot(step):
        return lax.rem(depth + step + ZS, ZS) * 2 + core

    up, down = (slot(1), ev), (slot(-1), ev)
    pair = (depth * 2 + 1 - core, ev)

    def sink_copy(a):
        return pltpu.make_async_copy(
            sink_ref.at[:, 0, :, a], sink_buf.at[a], sink_sem.at[a]
        )

    for a in range(BLOCK):
        sink_copy(a).start()

    barrier = pltpu.get_barrier_semaphore()
    for step in FAR_FIRST:
        pl.semaphore_signal(barrier, inc=1, device_id=(tm, peer(step)), device_id_type=MESH)
    for device in (up, down, pair):
        pl.semaphore_signal(barrier, inc=1, device_id=device, device_id_type=MESH)

    real, imag = peram_ref[0, 0], peram_ref[1, 0]
    real32, imag32 = real.astype(F32), imag.astype(F32)
    real_t, imag_t = real32.T.astype(BF16), imag32.T.astype(BF16)
    minus, minus_t = (-imag32).astype(BF16), (-imag32.T).astype(BF16)
    left_mat[...] = jnp.concatenate(
        [jnp.concatenate([real_t, minus_t], 1), jnp.concatenate([imag_t, real_t], 1)], 0
    )
    one = jnp.concatenate(
        [jnp.concatenate([real, imag], 1), jnp.concatenate([minus, real], 1)], 0
    )
    right_mat[...] = jnp.concatenate([one, one], 0)
    source_mat[...] = jnp.concatenate(
        [jnp.concatenate([real, minus], 1), jnp.concatenate([imag, real], 1)], 0
    )
    scale_own[...] = jnp.zeros_like(scale_own)

    def transform(a):
        scales = []
        for s2 in range(NS // 2):
            s = 2 * s2
            both = jnp.concatenate(
                [
                    jnp.concatenate([sink_buf[a, 0, s], sink_buf[a, 0, s + 1]], 1),
                    jnp.concatenate([sink_buf[a, 1, s], sink_buf[a, 1, s + 1]], 1),
                ],
                0,
            )
            once = lax.dot_general(left_mat[...], both, NN, preferred_element_type=F32)
            high, low = split_parts(once)
            lines = []
            for h in range(2):
                lanes = slice(h * NEV, (h + 1) * NEV)
                lines.append(
                    jnp.concatenate(
                        [high[:NEV, lanes], high[NEV:, lanes], low[:NEV, lanes], low[NEV:, lanes]], 1
                    )
                )
            twice = lax.dot_general(
                jnp.concatenate(lines, 0), right_mat[...], NN, preferred_element_type=F32
            )
            for h in range(2):
                mine = twice[h * NEV : (h + 1) * NEV]
                top = jnp.maximum(jnp.max(jnp.abs(mine), keepdims=True), 1e-35)
                code = jnp.round(mine * (TOP / top)).astype(jnp.int32)
                packed = (code[:, :NEV] << 16) | (code[:, NEV:] & 0xFFFF)
                send[:, a, pl.ds((s + h) * BLOCK, BLOCK), :] = packed.reshape(EV, BLOCK, NEV)
                scales.append(top * (1.0 / TOP))
        scales = jnp.concatenate(scales, 0)
        scale_own[...] = jnp.where(iota((NS, NEV), 1) == a, scales, scale_own[...])

    def send_copy(a, step):
        there = peer(step)
        return pltpu.make_async_remote_copy(
            send.at[there, a], recv.at[a, ev], send_sem.at[a], recv_sem.at[a],
            device_id=(tm, there), device_id_type=MESH,
        )

    def own_copy(a):
        return pltpu.make_async_copy(send.at[ev, a], recv.at[a, ev], own_sem.at[a])

    def post(a):
        for step in FAR_FIRST:
            send_copy(a, step).start()
        own_copy(a).start()

    def ring_copy(way, step):
        there = (up, down)[way]
        index = slot(-step) if way == 0 else slot(step)
        if step == 0:
            src, dst = source_ref, gathered.at[index]
        elif step < 3:
            src, dst = gathered.at[index], gathered.at[index]
        else:
            src, dst = gathered.at[index, way], gathered.at[index, way]
        return pltpu.make_async_remote_copy(
            src, dst, ring_sem.at[0, way, step], ring_sem.at[1, way, step],
            device_id=there, device_id_type=MESH,
        )

    def ring_arrival(way, step):
        index = slot(-step - 1) if way == 0 else slot(step + 1)
        ref = gathered.at[index] if step < 3 else gathered.at[index, way]
        return pltpu.make_async_copy(ref, ref, ring_sem.at[1, way, step])

    def pair_copy(order):
        step = (0, -1, 1, -2, 2, -3, 3, 4)[order]
        index = slot(step)
        src = source_ref if order == 0 else gathered.at[index]
        return pltpu.make_async_remote_copy(
            src, gathered.at[index], pair_sem.at[0, order], pair_sem.at[1, order],
            device_id=pair, device_id_type=MESH,
        )

    def pair_arrival(order):
        step = (0, -1, 1, -2, 2, -3, 3, 4)[order]
        index = lax.rem(depth + step + ZS, ZS) * 2 + 1 - core
        ref = gathered.at[index]
        return pltpu.make_async_copy(ref, ref, pair_sem.at[1, order])

    sink_copy(0).wait()
    transform(0)
    pl.semaphore_wait(barrier, EV - 1 + 3)
    for way in range(2):
        ring_copy(way, 0).start()
    pair_copy(0).start()
    mine_copy = pltpu.make_async_copy(source_ref, gathered.at[tm], slot_sem)
    mine_copy.start()
    post(0)

    @pl.loop(1, BLOCK)
    def _(a):
        sink_copy(a).wait()
        transform(a)
        post(a)

    def scale_copy(step):
        return pltpu.make_async_remote_copy(
            scale_own, scale_recv.at[ev], scale_sem.at[0], scale_sem.at[1],
            device_id=(tm, peer(step)), device_id_type=MESH,
        )

    for step in FAR_FIRST:
        scale_copy(step).start()

    def place(first):
        nucleon = first // 2
        return (
            perm_ref[nucleon : nucleon + 1, :] * NS + ops_ref[first : first + 1, :]
        ) * NS + ops_ref[first + 1 : first + 2, :]

    phase = jnp.where(time_ref[...] == tm, 1 - 2 * sign_ref[...], 0).astype(F32)
    entries = iota((NEV, phase.shape[1]), 0)
    first_hot = jnp.where(entries == place(0), phase, 0.0).astype(BF16)
    second_hot = jnp.where(entries == place(2), 1.0, 0.0).astype(BF16)
    counts[...] = lax.dot_general(first_hot, second_hot, NT, preferred_element_type=F32)

    for step in range(4):
        for way in range(2):
            ring_arrival(way, step).wait()
        if step < 3:
            for way in range(2):
                ring_copy(way, step + 1).start()
                pair_copy(2 * step + 1 + way).start()
        else:
            pair_copy(7).start()
    mine_copy.wait()
    for order in range(8):
        pair_arrival(order).wait()

    @pl.loop(0, NS)
    def _(u):
        for j2 in range(BLOCK // 2):
            mats = []
            for part in range(2):
                lines = gathered[:, part, u, pl.ds(j2 * 2 * BLOCK, 2 * BLOCK), :].astype(F32)
                mats.append(
                    [
                        lines[:, h * BLOCK : (h + 1) * BLOCK].reshape(NEV, NEV).astype(BF16)
                        for h in range(2)
                    ]
                )
            by_rows = jnp.concatenate(
                [jnp.concatenate([mats[0][h], mats[1][h]], 1) for h in range(2)], 0
            )
            by_lanes = jnp.concatenate(
                [jnp.concatenate([mats[part][0], mats[part][1]], 1) for part in range(2)], 0
            )
            direct = lax.dot_general(source_mat[...], by_rows, NT, preferred_element_type=F32)
            crossed = lax.dot_general(source_mat[...], by_lanes, NN, preferred_element_type=F32)
            for p, result in enumerate((direct, crossed)):
                for h in range(2):
                    at = (p * BLOCK + 2 * j2 + h) * 2 * NEV
                    stage[pl.ds(at, 2 * NEV), :] = result[:, h * NEV : (h + 1) * NEV]

        @pl.loop(0, EV)
        def _(block):
            lanes = pl.ds(pl.multiple_of(block * NEV, NEV), NEV)
            for p in range(2):
                for a in range(BLOCK):
                    tiles = []
                    for part in range(2):
                        at = p * BLOCK * 2 * NEV + part * NEV + a + block * BLOCK
                        value = stage[pl.ds(at, BLOCK, stride=2 * NEV), :]
                        high = value.astype(BF16).astype(F32)
                        tiles += [value, value - high]
                    rows = pl.ds(pl.multiple_of((p * NS + u) * 32, 32), 32)
                    rmat[a, rows, lanes] = jnp.concatenate(tiles, 0).astype(BF16)

    for step in FAR_FIRST[:1]:
        pltpu.make_async_copy(
            scale_recv.at[pl.ds(0, EV - 1)], scale_recv.at[pl.ds(0, EV - 1)], scale_sem.at[1]
        ).wait()
    scale_recv[ev] = scale_own[...]

    @pl.loop(0, EV)
    def _(block):
        tile = scale_recv[block]
        for a in range(BLOCK):
            scale_wide[a, block] = jnp.broadcast_to(tile[:, a : a + 1], (NS, NEV))

    total[...] = jnp.zeros_like(total)

    @pl.loop(0, BLOCK)
    def _(a):
        own_copy(a).wait()
        pltpu.make_async_copy(
            recv.at[a, pl.ds(0, EV - 1)], recv.at[a, pl.ds(0, EV - 1)], recv_sem.at[a]
        ).wait()

        @pl.loop(0, EV)
        def _(block):
            lanes = pl.ds(pl.multiple_of(block * NEV, NEV), NEV)
            scale = jnp.broadcast_to(
                scale_wide[a, block][:, None, :], (NS, BLOCK, NEV)
            ).reshape(ROWS, NEV)
            packed = recv[a, block]
            real_high, real_low = split_parts((packed >> 16).astype(F32) * scale)
            imag_high, imag_low = split_parts(((packed << 16) >> 16).astype(F32) * scale)
            tmat[:, lanes] = jnp.concatenate([real_high, real_low, imag_high, imag_low], 0)

        total[...] += lax.dot_general(rmat[a], tmat[...], NT, preferred_element_type=F32)

    alike = (iota((512, 256), 0) % BLOCK) == (iota((512, 256), 1) % BLOCK)
    kept = jnp.where(alike, total[...], 0.0).reshape(32, 16, 256).sum(axis=1)
    source_row, entry = iota((256, 256), 0), iota((256, 256), 1)
    spread = (source_row // 128 == entry // 128) & (
        (source_row // BLOCK) % NS == (entry % 128) // NS % NS
    )
    lined = lax.dot_general(
        kept, jnp.where(spread, 1.0, 0.0), NN,
        precision=lax.Precision.HIGHEST, preferred_element_type=F32,
    )
    line, entry = iota((32, 128), 0), iota((32, 128), 1)
    wanted = (line // 16 == entry // 64) & (line // 2 % NS == entry % NS)
    real_line = line % 2 == 0
    with_real, with_imag = lined[:, :NEV], lined[:, NEV:]
    real_sum = jnp.where(wanted, jnp.where(real_line, with_real, -with_imag), 0.0)
    imag_sum = jnp.where(wanted, jnp.where(real_line, with_imag, with_real), 0.0)
    part_own[...] = jnp.concatenate(
        [real_sum.sum(axis=0, keepdims=True), imag_sum.sum(axis=0, keepdims=True)], 0
    )

    def part_copy(step):
        return pltpu.make_async_remote_copy(
            part_own, part_recv.at[ev], part_sem.at[0], part_sem.at[1],
            device_id=(tm, peer(step)), device_id_type=MESH,
        )

    for step in FAR_FIRST:
        part_copy(step).start()
    part_recv[ev] = part_own[...]
    pltpu.make_async_copy(
        part_recv.at[pl.ds(0, EV - 1)], part_recv.at[pl.ds(0, EV - 1)], part_sem.at[1]
    ).wait()
    blocks = part_recv[0]
    for block in range(1, EV):
        blocks = blocks + part_recv[block]
    blocks = blocks * NEV ** (-1.5)
    blocks_ref[...] = blocks
    met = lax.dot_general(
        blocks, counts[...], NN, precision=lax.Precision.HIGHEST, preferred_element_type=F32
    )
    real_value = met[0:1] * blocks[0:1] - met[1:2] * blocks[1:2]
    imag_value = met[0:1] * blocks[1:2] + met[1:2] * blocks[0:1]
    value = jnp.concatenate([real_value, imag_value], 0).sum(axis=1, keepdims=True)
    corr_ref[...] = jnp.broadcast_to(value / math.sqrt(DIAG_T), corr_ref.shape)

    @pl.loop(0, BLOCK)
    def _(a):
        pltpu.make_async_copy(
            recv.at[a, pl.ds(0, EV - 1)], recv.at[a, pl.ds(0, EV - 1)], send_sem.at[a]
        ).wait()

    pltpu.make_async_copy(
        scale_recv.at[pl.ds(0, EV - 1)], scale_recv.at[pl.ds(0, EV - 1)], scale_sem.at[0]
    ).wait()
    pltpu.make_async_copy(
        part_recv.at[pl.ds(0, EV - 1)], part_recv.at[pl.ds(0, EV - 1)], part_sem.at[0]
    ).wait()
    for step in range(4):
        for way in range(2):
            ring_copy(way, step).wait_send()
    for order in range(8):
        pair_copy(order).wait_send()


def shards(
    sink_elemental,
    source_elemental,
    perambulator,
    diagram_time,
    diagram_perm,
    diagram_ops,
    diagram_sign,
):
    source = jnp.transpose(source_elemental, (0, 1, 3, 4, 2)).reshape(2, NS, ROWS, NEV)
    count = diagram_time.shape[0]
    whole = pl.BlockSpec(memory_space=pl.ANY)
    near = pl.BlockSpec(memory_space=pltpu.VMEM)
    dma = pltpu.SemaphoreType.DMA
    blocks, correlator = pl.pallas_call(
        kernel,
        out_shape=(
            jax.ShapeDtypeStruct((2, NEV), F32),
            jax.ShapeDtypeStruct((2, NEV), F32),
        ),
        in_specs=[whole, whole, near, near, near, near, near],
        out_specs=(near, near),
        scratch_shapes=[
            pltpu.VMEM((BLOCK, 2, NS, NEV, NEV), BF16),
            pltpu.VMEM((EV, BLOCK, ROWS, NEV), jnp.int32),
            pltpu.VMEM((BLOCK, EV, ROWS, NEV), jnp.int32),
            pltpu.VMEM((TM, 2, NS, ROWS, NEV), BF16),
            pltpu.VMEM((BLOCK, 512, EV * NEV), BF16),
            pltpu.VMEM((2 * BLOCK * 2 * NEV, NEV), F32),
            pltpu.VMEM((256, EV * NEV), BF16),
            pltpu.VMEM((512, 256), F32),
            pltpu.VMEM((NS, NEV), F32),
            pltpu.VMEM((EV, NS, NEV), F32),
            pltpu.VMEM((BLOCK, EV, NS, NEV), F32),
            pltpu.VMEM((256, 256), BF16),
            pltpu.VMEM((512, 256), BF16),
            pltpu.VMEM((256, 256), BF16),
            pltpu.VMEM((NEV, NEV), F32),
            pltpu.VMEM((2, NEV), F32),
            pltpu.VMEM((EV, 2, NEV), F32),
            dma((BLOCK,)),
            dma((BLOCK,)),
            dma((BLOCK,)),
            dma((BLOCK,)),
            dma((2,)),
            dma((2,)),
            dma((2, 2, 4)),
            dma((2, 8)),
            dma,
        ],
        compiler_params=pltpu.CompilerParams(
            collective_id=0, has_side_effects=True, vmem_limit_bytes=60 << 20
        ),
        cost_estimate=pl.CostEstimate(
            flops=17 * 10**9, bytes_accessed=5 << 20, transcendentals=0
        ),
    )(
        sink_elemental,
        source,
        perambulator,
        diagram_time.reshape(1, count),
        diagram_perm.T,
        diagram_ops.T,
        diagram_sign.reshape(1, count),
    )
    return blocks.reshape(2, 1, 2, NS, NS), correlator[:, :1]


def solution(mesh):
    placed = (
        P(None, "tm", None, "evec", None, None),
        P(None, None, None, "evec", "tm"),
        P(None, "tm", None, None),
        P(),
        P(),
        P(),
        P(),
    )
    return jax.shard_map(
        shards,
        mesh=mesh,
        in_specs=placed,
        out_specs=(P(None, "tm", None, None, None), P(None, "tm")),
        check_vma=False,
    )
```

```python
import functools
import math

import jax
import jax.numpy as jnp
from jax import lax
from jax.experimental import pallas as pl
from jax.experimental.pallas import tpu as pltpu
from jax.sharding import PartitionSpec as P

DIAG_T = 64
NEV = 128
NS = 8
BLOCK = 8
EV = 16
TM = 16
ZS = 8
ROWS = NS * BLOCK
RINGS = 7
TOP = 32767.0
MESH = pl.DeviceIdType.MESH
F32 = jnp.float32
BF16 = jnp.bfloat16
NT = (((1,), (1,)), ((), ()))
NN = (((1,), (0,)), ((), ()))
FAR_FIRST = (10, 9, 11, 6, 14, 2, 8, 5, 7, 13, 15, 1, 3, 4, 12)


def split_parts(value):
    high = value.astype(BF16)
    return high, (value - high.astype(F32)).astype(BF16)


def iota(shape, axis):
    return lax.broadcasted_iota(jnp.int32, shape, axis)


def kernel(
    sink_ref,
    source_ref,
    peram_ref,
    time_ref,
    perm_ref,
    ops_ref,
    sign_ref,
    blocks_ref,
    corr_ref,
    sink_buf,
    send,
    recv,
    gathered,
    rmat,
    stage,
    tmat,
    total,
    scale_own,
    scale_recv,
    wide,
    left_mat,
    right_mat,
    source_mat,
    counts,
    spread,
    part_own,
    part_recv,
    sink_sem,
    send_sem,
    recv_sem,
    own_sem,
    scale_sem,
    part_sem,
    ring_sem,
    pair_sem,
    first_sem,
    slot_sem,
):
    tm = lax.axis_index("tm")
    ev = lax.axis_index("evec")
    row, column = ev // 4, lax.rem(ev, 4)
    depth, core = tm // 2, lax.rem(tm, 2)

    def peer(step):
        return lax.rem(row + step // 4, 4) * 4 + lax.rem(column + step % 4, 4)

    def slot(step):
        return lax.rem(depth + step + ZS, ZS) * 2 + core

    up, down = (slot(1), ev), (slot(-1), ev)
    pair = (depth * 2 + 1 - core, ev)

    def sink_copy(a):
        return pltpu.make_async_copy(
            sink_ref.at[:, 0, :, a], sink_buf.at[a], sink_sem.at[a]
        )

    for a in range(BLOCK):
        sink_copy(a).start()

    barrier = pltpu.get_barrier_semaphore()
    for step in FAR_FIRST:
        pl.semaphore_signal(barrier, inc=1, device_id=(tm, peer(step)), device_id_type=MESH)
    for device in (up, down, pair):
        pl.semaphore_signal(barrier, inc=1, device_id=device, device_id_type=MESH)

    real, imag = peram_ref[0, 0], peram_ref[1, 0]
    real32, imag32 = real.astype(F32), imag.astype(F32)
    real_t, imag_t = real32.T.astype(BF16), imag32.T.astype(BF16)
    minus, minus_t = (-imag32).astype(BF16), (-imag32.T).astype(BF16)
    left_mat[...] = jnp.concatenate(
        [jnp.concatenate([real_t, minus_t], 1), jnp.concatenate([imag_t, real_t], 1)], 0
    )
    one = jnp.concatenate(
        [jnp.concatenate([real, imag], 1), jnp.concatenate([minus, real], 1)], 0
    )
    right_mat[...] = jnp.concatenate([one, one], 0)
    source_mat[...] = jnp.concatenate(
        [jnp.concatenate([real, minus], 1), jnp.concatenate([imag, real], 1)], 0
    )

    def transform(a):
        for s2 in range(NS // 2):
            s = 2 * s2
            both = jnp.concatenate(
                [
                    jnp.concatenate([sink_buf[a, 0, s], sink_buf[a, 0, s + 1]], 1),
                    jnp.concatenate([sink_buf[a, 1, s], sink_buf[a, 1, s + 1]], 1),
                ],
                0,
            )
            once = lax.dot_general(left_mat[...], both, NN, preferred_element_type=F32)
            high, low = split_parts(once)
            lines = []
            for h in range(2):
                lanes = slice(h * NEV, (h + 1) * NEV)
                lines.append(
                    jnp.concatenate(
                        [high[:NEV, lanes], high[NEV:, lanes], low[:NEV, lanes], low[NEV:, lanes]], 1
                    )
                )
            wide[pl.ds(s * NEV, 2 * NEV), :] = lax.dot_general(
                jnp.concatenate(lines, 0), right_mat[...], NN, preferred_element_type=F32
            )
        for there in range(EV):
            value = jnp.concatenate(
                [wide[pl.ds(s * NEV + there * BLOCK, BLOCK), :] for s in range(NS)], 0
            )
            top = jnp.max(jnp.abs(value), axis=0, keepdims=True)
            top = jnp.maximum(jnp.maximum(top[:, :NEV], top[:, NEV:]), 1e-35)
            factor = TOP / top
            real_code = jnp.round(value[:, :NEV] * factor).astype(jnp.int32)
            imag_code = jnp.round(value[:, NEV:] * factor).astype(jnp.int32)
            send[there, a] = (real_code << 16) | (imag_code & 0xFFFF)
            scale_own[there, a] = top * (1.0 / TOP)

    def send_copy(a, step):
        there = peer(step)
        return pltpu.make_async_remote_copy(
            send.at[there, a], recv.at[a, ev], send_sem.at[a], recv_sem.at[a],
            device_id=(tm, there), device_id_type=MESH,
        )

    def scale_copy(a, step):
        there = peer(step)
        return pltpu.make_async_remote_copy(
            scale_own.at[there, a], scale_recv.at[a, ev], scale_sem.at[0, a], scale_sem.at[1, a],
            device_id=(tm, there), device_id_type=MESH,
        )

    def own_copy(a):
        return pltpu.make_async_copy(send.at[ev, a], recv.at[a, ev], own_sem.at[a])

    def post(a):
        for step in FAR_FIRST:
            scale_copy(a, step).start()
            send_copy(a, step).start()
        own_copy(a).start()
        scale_recv[a, ev] = scale_own[ev, a]

    def arrived(ref, sem):
        pltpu.make_async_copy(ref, ref, sem).wait()

    def ring_copy(way, message):
        step, half = message // 2, lax.rem(message + way, 2)
        index = slot(step * (2 * way - 1))
        src = source_ref.at[half] if isinstance(message, int) else gathered.at[index, half]
        return pltpu.make_async_remote_copy(
            src, gathered.at[index, half], ring_sem.at[0, way, message],
            ring_sem.at[1, way, message], device_id=(up, down)[way], device_id_type=MESH,
        )

    def ring_arrival(way, message):
        index = slot((message // 2 + 1) * (2 * way - 1))
        return gathered.at[index, lax.rem(message + way, 2)]

    def pair_copy(way, message):
        ref = ring_arrival(way, message)
        return pltpu.make_async_remote_copy(
            ref, ref, pair_sem.at[0, way, message], pair_sem.at[1, way, message],
            device_id=pair, device_id_type=MESH,
        )

    def pair_arrival(way, message):
        index = slot((message // 2 + 1) * (2 * way - 1)) + 1 - 2 * core
        return gathered.at[index, lax.rem(message + way, 2)]

    pair_first = pltpu.make_async_remote_copy(
        source_ref, gathered.at[tm], first_sem.at[0], first_sem.at[1],
        device_id=pair, device_id_type=MESH,
    )
    own_source = pltpu.make_async_copy(source_ref, gathered.at[tm], slot_sem)

    def relay(message):
        for way in range(2):
            arrived(ring_arrival(way, message), ring_sem.at[1, way, message])
            pair_copy(way, message).start()

        @pl.when(message < 4)
        def _():
            for way in range(2):
                ring_copy(way, message + 2).start()

        @pl.when(message == 4)
        def _():
            ring_copy(0, message + 2).start()

        @pl.when(message == 5)
        def _():
            ring_copy(1, message + 1).start()

    own_source.start()
    pl.semaphore_wait(barrier, EV - 1 + 3)
    for message in range(2):
        for way in range(2):
            ring_copy(way, message).start()
    pair_first.start()
    sink_copy(0).wait()
    transform(0)
    post(0)

    @pl.loop(1, BLOCK)
    def _(a):
        sink_copy(a).wait()
        transform(a)
        post(a)
        relay(a - 1)

    def position(first):
        nucleon = first // 2
        return (
            perm_ref[nucleon : nucleon + 1, :] * NS + ops_ref[first : first + 1, :]
        ) * NS + ops_ref[first + 1 : first + 2, :]

    phase = jnp.where(time_ref[...] == tm, 1 - 2 * sign_ref[...], 0).astype(F32)
    entries = iota((NEV, phase.shape[1]), 0)
    first_hot = jnp.where(entries == position(0), phase, 0.0).astype(BF16)
    second_hot = jnp.where(entries == position(2), 1.0, 0.0).astype(BF16)
    counts[...] = lax.dot_general(first_hot, second_hot, NT, preferred_element_type=F32)

    own_source.wait()
    arrived(gathered.at[tm + 1 - 2 * core], first_sem.at[1])

    @pl.loop(0, RINGS)
    def _(message):
        for way in range(2):
            arrived(pair_arrival(way, message), pair_sem.at[1, way, message])

    @pl.loop(0, NS)
    def _(u):
        for j2 in range(BLOCK // 2):
            mats = []
            for part in range(2):
                lines = gathered[:, part, u, pl.ds(j2 * 2 * BLOCK, 2 * BLOCK), :].astype(F32)
                mats.append(
                    [
                        lines[:, h * BLOCK : (h + 1) * BLOCK].reshape(NEV, NEV).astype(BF16)
                        for h in range(2)
                    ]
                )
            by_rows = jnp.concatenate(
                [jnp.concatenate([mats[0][h], mats[1][h]], 1) for h in range(2)], 0
            )
            by_lanes = jnp.concatenate(
                [jnp.concatenate([mats[part][0], mats[part][1]], 1) for part in range(2)], 0
            )
            direct = lax.dot_general(source_mat[...], by_rows, NT, preferred_element_type=F32)
            crossed = lax.dot_general(source_mat[...], by_lanes, NN, preferred_element_type=F32)
            for p, result in enumerate((direct, crossed)):
                for h in range(2):
                    at = (p * BLOCK + 2 * j2 + h) * 2 * NEV
                    stage[pl.ds(at, 2 * NEV), :] = result[:, h * NEV : (h + 1) * NEV]

        @pl.loop(0, EV)
        def _(block):
            lanes = pl.ds(pl.multiple_of(block * NEV, NEV), NEV)
            for p in range(2):
                turned = []
                for part in range(2):
                    tiles = [
                        stage[
                            pl.ds((p * BLOCK + j) * 2 * NEV + part * NEV + block * BLOCK, BLOCK), :
                        ]
                        for j in range(BLOCK)
                    ]
                    turned.append(jnp.swapaxes(jnp.stack(tiles, 0), 0, 1))
                rows = pl.ds(pl.multiple_of((p * NS + u) * 32, 32), 32)
                for a in range(BLOCK):
                    parts = []
                    for part in range(2):
                        value = turned[part][a]
                        parts += [value, value - value.astype(BF16).astype(F32)]
                    rmat[a, rows, lanes] = jnp.concatenate(parts, 0).astype(BF16)

    total[...] = jnp.zeros_like(total)
    tile_row, entry = iota((256, 256), 0), iota((256, 256), 1)
    spread[...] = jnp.where(
        (tile_row // 128 == entry // 128) & (tile_row // BLOCK % NS == entry // NS % NS), 1.0, 0.0
    ).astype(BF16)

    others = pl.ds(0, EV - 1)

    @pl.loop(0, BLOCK)
    def _(a):
        own_copy(a).wait()
        arrived(scale_recv.at[a, others], scale_sem.at[1, a])
        arrived(recv.at[a, others], recv_sem.at[a])
        for block in range(EV):
            scale = scale_recv[a, block]
            packed = recv[a, block]
            real_high, real_low = split_parts((packed >> 16).astype(F32) * scale)
            imag_high, imag_low = split_parts(((packed << 16) >> 16).astype(F32) * scale)
            tmat[:, block * NEV : (block + 1) * NEV] = jnp.concatenate(
                [real_high, real_low, imag_high, imag_low], 0
            )
        total[...] += lax.dot_general(rmat[a], tmat[...], NT, preferred_element_type=F32)

    alike = (iota((512, 256), 0) % BLOCK) == (iota((512, 256), 1) % BLOCK)
    kept = jnp.where(alike, total[...], 0.0).reshape(32, 16, 256).sum(axis=1)
    high = kept.astype(BF16)
    rest = kept - high.astype(F32)
    middle, low = split_parts(rest)
    lined = lax.dot_general(
        jnp.concatenate([high, middle, low], 0), spread[...], NN, preferred_element_type=F32
    ).reshape(3, 32, 256)
    lined = lined[0] + (lined[1] + lined[2])
    line, entry = iota((32, 128), 0), iota((32, 128), 1)
    wanted = (line // 16 == entry // 64) & (line // 2 % NS == entry % NS)
    real_line = line % 2 == 0
    with_real, with_imag = lined[:, :NEV], lined[:, NEV:]
    real_sum = jnp.where(wanted, jnp.where(real_line, with_real, -with_imag), 0.0)
    imag_sum = jnp.where(wanted, jnp.where(real_line, with_imag, with_real), 0.0)
    part_own[...] = jnp.concatenate(
        [real_sum.sum(axis=0, keepdims=True), imag_sum.sum(axis=0, keepdims=True)], 0
    )

    def part_copy(step):
        return pltpu.make_async_remote_copy(
            part_own, part_recv.at[ev], part_sem.at[0], part_sem.at[1],
            device_id=(tm, peer(step)), device_id_type=MESH,
        )

    for step in FAR_FIRST:
        part_copy(step).start()
    part_recv[ev] = part_own[...]
    arrived(part_recv.at[others], part_sem.at[1])
    blocks = part_recv[0]
    for block in range(1, EV):
        blocks = blocks + part_recv[block]
    blocks = blocks * NEV ** (-1.5)
    line, entry = iota((32, NEV), 0), iota((32, NEV), 1)
    lines = jnp.concatenate(
        [jnp.broadcast_to(blocks[part : part + 1], (16, NEV)) for part in range(2)], 0
    )
    lines = jnp.where(line % 16 == entry // NS, lines, 0.0)
    picked = iota((NEV, NS), 0) % NS == iota((NEV, NS), 1)
    blocks_ref[...] = lax.dot_general(
        lines, jnp.where(picked, 1.0, 0.0), NN,
        precision=lax.Precision.HIGHEST, preferred_element_type=F32,
    ).reshape(blocks_ref.shape)
    met = lax.dot_general(
        blocks, counts[...], NN, precision=lax.Precision.HIGHEST, preferred_element_type=F32
    )
    real_value = met[0:1] * blocks[0:1] - met[1:2] * blocks[1:2]
    imag_value = met[0:1] * blocks[1:2] + met[1:2] * blocks[0:1]
    value = [part.sum(axis=1, keepdims=True) for part in (real_value, imag_value)]
    corr_ref[...] = jnp.concatenate(value, 1) / math.sqrt(DIAG_T)

    @pl.loop(0, BLOCK)
    def _(a):
        arrived(recv.at[a, others], send_sem.at[a])
        arrived(scale_recv.at[a, others], scale_sem.at[0, a])

    arrived(part_recv.at[others], part_sem.at[0])
    pair_first.wait_send()

    @pl.loop(0, RINGS)
    def _(message):
        for way in range(2):
            arrived(pair_arrival(way, message), ring_sem.at[0, way, message])
            arrived(pair_arrival(way, message), pair_sem.at[0, way, message])


def place(blocks_in, corr_in, blocks_ref, corr_ref):
    blocks_ref[...] = blocks_in[...]
    corr_ref[...] = corr_in[...]


def shards(
    sink_elemental,
    source_elemental,
    perambulator,
    diagram_time,
    diagram_perm,
    diagram_ops,
    diagram_sign,
):
    source = jnp.transpose(source_elemental, (0, 1, 3, 4, 2)).reshape(2, NS, ROWS, NEV)
    count = diagram_time.shape[0]
    whole = pl.BlockSpec(memory_space=pl.ANY)
    near = pl.BlockSpec(memory_space=pltpu.VMEM)
    dma = pltpu.SemaphoreType.DMA
    blocks, correlator = pl.pallas_call(
        kernel,
        out_shape=(
            jax.ShapeDtypeStruct((2, 1, 2, NS, NS), F32),
            jax.ShapeDtypeStruct((1, 2), F32),
        ),
        in_specs=[whole, whole, near, near, near, near, near],
        out_specs=(near, near),
        scratch_shapes=[
            pltpu.VMEM((BLOCK, 2, NS, NEV, NEV), BF16),
            pltpu.VMEM((EV, BLOCK, ROWS, NEV), jnp.int32),
            pltpu.VMEM((BLOCK, EV, ROWS, NEV), jnp.int32),
            pltpu.VMEM((TM, 2, NS, ROWS, NEV), BF16),
            pltpu.VMEM((BLOCK, 512, EV * NEV), BF16),
            pltpu.VMEM((2 * BLOCK * 2 * NEV, NEV), F32),
            pltpu.VMEM((256, EV * NEV), BF16),
            pltpu.VMEM((512, 256), F32),
            pltpu.VMEM((EV, BLOCK, 1, NEV), F32),
            pltpu.VMEM((BLOCK, EV, 1, NEV), F32),
            pltpu.VMEM((NS * NEV, 2 * NEV), F32),
            pltpu.VMEM((256, 256), BF16),
            pltpu.VMEM((512, 256), BF16),
            pltpu.VMEM((256, 256), BF16),
            pltpu.VMEM((NEV, NEV), F32),
            pltpu.VMEM((256, 256), BF16),
            pltpu.VMEM((2, NEV), F32),
            pltpu.VMEM((EV, 2, NEV), F32),
            dma((BLOCK,)),
            dma((BLOCK,)),
            dma((BLOCK,)),
            dma((BLOCK,)),
            dma((2, BLOCK)),
            dma((2,)),
            dma((2, 2, RINGS)),
            dma((2, 2, RINGS)),
            dma((2,)),
            dma,
        ],
        compiler_params=pltpu.CompilerParams(
            collective_id=0, has_side_effects=True, vmem_limit_bytes=60 << 20
        ),
        cost_estimate=pl.CostEstimate(
            flops=17 * 10**9, bytes_accessed=5 << 20, transcendentals=0
        ),
    )(
        sink_elemental,
        source,
        perambulator,
        diagram_time.reshape(1, count),
        diagram_perm.T,
        diagram_ops.T,
        diagram_sign.reshape(1, count),
    )
    blocks, correlator = pl.pallas_call(
        place,
        out_shape=(
            jax.ShapeDtypeStruct(blocks.shape, F32),
            jax.ShapeDtypeStruct(correlator.shape, F32),
        ),
        in_specs=[near, near],
        out_specs=(near, near),
    )(blocks, correlator)
    return blocks, correlator.T


def solution(mesh):
    placed = (
        P(None, "tm", None, "evec", None, None),
        P(None, None, None, "evec", "tm"),
        P(None, "tm", None, None),
        P(),
        P(),
        P(),
        P(),
    )
    return jax.shard_map(
        shards,
        mesh=mesh,
        in_specs=placed,
        out_specs=(P(None, "tm", None, None, None), P(None, "tm")),
        check_vma=False,
    )
```

```python
import functools
import math

import jax
import jax.numpy as jnp
from jax import lax
from jax.experimental import pallas as pl
from jax.experimental.pallas import tpu as pltpu
from jax.sharding import PartitionSpec as P

DIAG_T = 64
NEV = 128
NS = 8
BLOCK = 8
EV = 16
TM = 16
ZS = 8
ROWS = NS * BLOCK
RINGS = 7
TOP = 32767.0
MESH = pl.DeviceIdType.MESH
F32 = jnp.float32
BF16 = jnp.bfloat16
NT = (((1,), (1,)), ((), ()))
NN = (((1,), (0,)), ((), ()))
FAR_FIRST = (10, 9, 11, 6, 14, 2, 8, 5, 7, 13, 15, 1, 3, 4, 12)


def split_parts(value):
    high = value.astype(BF16)
    return high, (value - high.astype(F32)).astype(BF16)


def three_parts(value):
    high = value.astype(BF16)
    middle, low = split_parts(value - high.astype(F32))
    return jnp.concatenate([high, middle, low], 0)


def iota(shape, axis):
    return lax.broadcasted_iota(jnp.int32, shape, axis)


def kernel(
    sink_ref,
    source_ref,
    peram_in,
    time_in,
    perm_in,
    ops_in,
    sign_in,
    blocks_ref,
    corr_ref,
    peram_ref,
    time_ref,
    perm_ref,
    ops_ref,
    sign_ref,
    sink_buf,
    send,
    recv,
    gathered,
    rmat,
    stage,
    tmat,
    total,
    scale_own,
    scale_recv,
    wide,
    left_mat,
    right_mat,
    source_mat,
    counts,
    spread,
    part_own,
    part_recv,
    sink_sem,
    send_sem,
    recv_sem,
    own_sem,
    scale_sem,
    part_sem,
    ring_sem,
    pair_sem,
    first_sem,
    slot_sem,
    small_sem,
):
    tm = lax.axis_index("tm")
    ev = lax.axis_index("evec")
    row, column = ev // 4, lax.rem(ev, 4)
    depth, core = tm // 2, lax.rem(tm, 2)

    def peer(step):
        return lax.rem(row + step // 4, 4) * 4 + lax.rem(column + step % 4, 4)

    def slot(step):
        return lax.rem(depth + step + ZS, ZS) * 2 + core

    up, down = (slot(1), ev), (slot(-1), ev)
    pair = (depth * 2 + 1 - core, ev)

    def sink_copy(a):
        return pltpu.make_async_copy(
            sink_ref.at[:, 0, :, a], sink_buf.at[a], sink_sem.at[a]
        )

    small = [
        pltpu.make_async_copy(whole, near, small_sem.at[at])
        for at, (whole, near) in enumerate(
            (
                (peram_in, peram_ref),
                (time_in, time_ref),
                (perm_in, perm_ref),
                (ops_in, ops_ref),
                (sign_in, sign_ref),
            )
        )
    ]
    small[0].start()
    sink_copy(0).start()
    barrier = pltpu.get_barrier_semaphore()
    for step in FAR_FIRST:
        pl.semaphore_signal(barrier, inc=1, device_id=(tm, peer(step)), device_id_type=MESH)
    for device in (up, down, pair):
        pl.semaphore_signal(barrier, inc=1, device_id=device, device_id_type=MESH)
    for a in range(1, BLOCK):
        sink_copy(a).start()
    small[0].wait()

    real, imag = peram_ref[0, 0], peram_ref[1, 0]
    real32, imag32 = real.astype(F32), imag.astype(F32)
    real_t, imag_t = real32.T.astype(BF16), imag32.T.astype(BF16)
    minus, minus_t = (-imag32).astype(BF16), (-imag32.T).astype(BF16)
    left_mat[...] = jnp.concatenate(
        [jnp.concatenate([real_t, minus_t], 1), jnp.concatenate([imag_t, real_t], 1)], 0
    )
    one = jnp.concatenate(
        [jnp.concatenate([real, imag], 1), jnp.concatenate([minus, real], 1)], 0
    )
    right_mat[...] = jnp.concatenate([one, one], 0)
    source_mat[...] = jnp.concatenate(
        [jnp.concatenate([real, minus], 1), jnp.concatenate([imag, real], 1)], 0
    )

    def transform(a):
        for s2 in range(NS // 2):
            s = 2 * s2
            both = jnp.concatenate(
                [
                    jnp.concatenate([sink_buf[a, 0, s], sink_buf[a, 0, s + 1]], 1),
                    jnp.concatenate([sink_buf[a, 1, s], sink_buf[a, 1, s + 1]], 1),
                ],
                0,
            )
            once = lax.dot_general(left_mat[...], both, NN, preferred_element_type=F32)
            high, low = split_parts(once)
            lines = []
            for h in range(2):
                lanes = slice(h * NEV, (h + 1) * NEV)
                lines.append(
                    jnp.concatenate(
                        [high[:NEV, lanes], high[NEV:, lanes], low[:NEV, lanes], low[NEV:, lanes]], 1
                    )
                )
            wide[pl.ds(s * NEV, 2 * NEV), :] = lax.dot_general(
                jnp.concatenate(lines, 0), right_mat[...], NN, preferred_element_type=F32
            )
    def encode(a, there):
        value = jnp.concatenate(
            [
                wide[pl.ds(pl.multiple_of(s * NEV + there * BLOCK, BLOCK), BLOCK), :]
                for s in range(NS)
            ],
            0,
        )
        top = jnp.max(jnp.abs(value), axis=0, keepdims=True)
        top = jnp.maximum(jnp.maximum(top[:, :NEV], top[:, NEV:]), 1e-35)
        factor = TOP / top
        real_code = jnp.round(value[:, :NEV] * factor).astype(jnp.int32)
        imag_code = jnp.round(value[:, NEV:] * factor).astype(jnp.int32)
        send[there, a] = (real_code << 16) | (imag_code & 0xFFFF)
        scale_own[there, a] = top * (1.0 / TOP)

    def send_copy(a, step):
        there = peer(step)
        return pltpu.make_async_remote_copy(
            send.at[there, a], recv.at[a, ev], send_sem.at[a], recv_sem.at[a],
            device_id=(tm, there), device_id_type=MESH,
        )

    def scale_copy(a, step):
        there = peer(step)
        return pltpu.make_async_remote_copy(
            scale_own.at[there, a], scale_recv.at[a, ev], scale_sem.at[0, a], scale_sem.at[1, a],
            device_id=(tm, there), device_id_type=MESH,
        )

    def own_copy(a):
        return pltpu.make_async_copy(send.at[ev, a], recv.at[a, ev], own_sem.at[a])

    def post(a):
        for step in FAR_FIRST:
            encode(a, peer(step))
            scale_copy(a, step).start()
            send_copy(a, step).start()
        encode(a, ev)
        own_copy(a).start()
        scale_recv[a, ev] = scale_own[ev, a]

    def arrived(ref, sem):
        pltpu.make_async_copy(ref, ref, sem).wait()

    def ring_copy(way, message):
        step, half = message // 2, lax.rem(message + way, 2)
        index = slot(step * (2 * way - 1))
        src = source_ref.at[half] if isinstance(message, int) else gathered.at[index, half]
        return pltpu.make_async_remote_copy(
            src, gathered.at[index, half], ring_sem.at[0, way, message],
            ring_sem.at[1, way, message], device_id=(up, down)[way], device_id_type=MESH,
        )

    def ring_arrival(way, message):
        index = slot((message // 2 + 1) * (2 * way - 1))
        return gathered.at[index, lax.rem(message + way, 2)]

    def pair_copy(way, message):
        ref = ring_arrival(way, message)
        return pltpu.make_async_remote_copy(
            ref, ref, pair_sem.at[0, way, message], pair_sem.at[1, way, message],
            device_id=pair, device_id_type=MESH,
        )

    def pair_arrival(way, message):
        index = slot((message // 2 + 1) * (2 * way - 1)) + 1 - 2 * core
        return gathered.at[index, lax.rem(message + way, 2)]

    pair_first = pltpu.make_async_remote_copy(
        source_ref, gathered.at[tm], first_sem.at[0], first_sem.at[1],
        device_id=pair, device_id_type=MESH,
    )
    own_source = pltpu.make_async_copy(source_ref, gathered.at[tm], slot_sem)

    def relay(message):
        for way in range(2):
            arrived(ring_arrival(way, message), ring_sem.at[1, way, message])
            pair_copy(way, message).start()

        @pl.when(message < 4)
        def _():
            for way in range(2):
                ring_copy(way, message + 2).start()

        @pl.when(message == 4)
        def _():
            ring_copy(0, message + 2).start()

        @pl.when(message == 5)
        def _():
            ring_copy(1, message + 1).start()

    pl.semaphore_wait(barrier, EV - 1 + 3)
    for message in range(2):
        for way in range(2):
            ring_copy(way, message).start()
    pair_first.start()
    own_source.start()
    sink_copy(0).wait()
    transform(0)
    post(0)

    for copy in small[1:]:
        copy.start()

    @pl.loop(1, BLOCK)
    def _(a):
        sink_copy(a).wait()
        transform(a)
        post(a)
        relay(a - 1)

    def position(first):
        nucleon = first // 2
        return (
            perm_ref[nucleon : nucleon + 1, :] * NS + ops_ref[first : first + 1, :]
        ) * NS + ops_ref[first + 1 : first + 2, :]

    for copy in small[1:]:
        copy.wait()
    phase = jnp.where(time_ref[...] == tm, 1 - 2 * sign_ref[...], 0).astype(F32)
    entries = iota((NEV, phase.shape[1]), 0)
    first_hot = jnp.where(entries == position(0), phase, 0.0).astype(BF16)
    second_hot = jnp.where(entries == position(2), 1.0, 0.0).astype(BF16)
    counts[...] = jnp.concatenate(
        split_parts(
            lax.dot_general(first_hot, second_hot, NT, preferred_element_type=F32)
        ),
        1,
    )

    own_source.wait()
    arrived(gathered.at[tm + 1 - 2 * core], first_sem.at[1])

    @pl.loop(0, RINGS)
    def _(message):
        for way in range(2):
            arrived(pair_arrival(way, message), pair_sem.at[1, way, message])

    @pl.loop(0, NS)
    def _(u):
        for j2 in range(BLOCK // 2):
            mats = []
            for part in range(2):
                lines = gathered[:, part, u, pl.ds(j2 * 2 * BLOCK, 2 * BLOCK), :].astype(F32)
                mats.append(
                    [
                        lines[:, h * BLOCK : (h + 1) * BLOCK].reshape(NEV, NEV).astype(BF16)
                        for h in range(2)
                    ]
                )
            by_rows = jnp.concatenate(
                [jnp.concatenate([mats[0][h], mats[1][h]], 1) for h in range(2)], 0
            )
            by_lanes = jnp.concatenate(
                [jnp.concatenate([mats[part][0], mats[part][1]], 1) for part in range(2)], 0
            )
            direct = lax.dot_general(source_mat[...], by_rows, NT, preferred_element_type=F32)
            crossed = lax.dot_general(source_mat[...], by_lanes, NN, preferred_element_type=F32)
            for p, result in enumerate((direct, crossed)):
                for h in range(2):
                    at = (p * BLOCK + 2 * j2 + h) * 2 * NEV
                    stage[pl.ds(at, 2 * NEV), :] = result[:, h * NEV : (h + 1) * NEV]

        @pl.loop(0, EV)
        def _(block):
            lanes = pl.ds(pl.multiple_of(block * NEV, NEV), NEV)
            for p in range(2):
                turned = []
                for part in range(2):
                    tiles = [
                        stage[
                            pl.ds((p * BLOCK + j) * 2 * NEV + part * NEV + block * BLOCK, BLOCK), :
                        ]
                        for j in range(BLOCK)
                    ]
                    turned.append(jnp.swapaxes(jnp.stack(tiles, 0), 0, 1))
                rows = pl.ds(pl.multiple_of((p * NS + u) * 32, 32), 32)
                for a in range(BLOCK):
                    parts = []
                    for part in range(2):
                        value = turned[part][a]
                        parts += [value, value - value.astype(BF16).astype(F32)]
                    rmat[a, rows, lanes] = jnp.concatenate(parts, 0).astype(BF16)

    total[...] = jnp.zeros_like(total)
    tile_row, entry = iota((256, 256), 0), iota((256, 256), 1)
    spread[...] = jnp.where(
        (tile_row // 128 == entry // 128) & (tile_row // BLOCK % NS == entry // NS % NS), 1.0, 0.0
    ).astype(BF16)

    others = pl.ds(0, EV - 1)
    pair_first.wait_send()

    @pl.loop(0, RINGS)
    def _(message):
        for way in range(2):
            arrived(pair_arrival(way, message), ring_sem.at[0, way, message])
            arrived(pair_arrival(way, message), pair_sem.at[0, way, message])

    @pl.loop(0, BLOCK)
    def _(a):
        own_copy(a).wait()
        arrived(scale_recv.at[a, others], scale_sem.at[0, a])
        arrived(recv.at[a, others], send_sem.at[a])
        arrived(scale_recv.at[a, others], scale_sem.at[1, a])
        arrived(recv.at[a, others], recv_sem.at[a])
        for block in range(EV):
            scale = scale_recv[a, block]
            packed = recv[a, block]
            real_high, real_low = split_parts((packed >> 16).astype(F32) * scale)
            imag_high, imag_low = split_parts(((packed << 16) >> 16).astype(F32) * scale)
            tmat[:, block * NEV : (block + 1) * NEV] = jnp.concatenate(
                [real_high, real_low, imag_high, imag_low], 0
            )
        total[...] += lax.dot_general(rmat[a], tmat[...], NT, preferred_element_type=F32)

    alike = (iota((512, 256), 0) % BLOCK) == (iota((512, 256), 1) % BLOCK)
    kept = jnp.where(alike, total[...], 0.0).reshape(32, 16, 256).sum(axis=1)
    lined = lax.dot_general(
        three_parts(kept), spread[...], NN, preferred_element_type=F32
    ).reshape(3, 32, 256)
    lined = lined[0] + (lined[1] + lined[2])
    line, entry = iota((32, 128), 0), iota((32, 128), 1)
    wanted = (line // 16 == entry // 64) & (line // 2 % NS == entry % NS)
    real_line = line % 2 == 0
    with_real, with_imag = lined[:, :NEV], lined[:, NEV:]
    real_sum = jnp.where(wanted, jnp.where(real_line, with_real, -with_imag), 0.0)
    imag_sum = jnp.where(wanted, jnp.where(real_line, with_imag, with_real), 0.0)
    part_own[...] = jnp.concatenate(
        [real_sum.sum(axis=0, keepdims=True), imag_sum.sum(axis=0, keepdims=True)], 0
    )

    def part_copy(step):
        return pltpu.make_async_remote_copy(
            part_own, part_recv.at[ev], part_sem.at[0], part_sem.at[1],
            device_id=(tm, peer(step)), device_id_type=MESH,
        )

    for step in FAR_FIRST:
        part_copy(step).start()
    part_recv[ev] = part_own[...]
    arrived(part_recv.at[others], part_sem.at[1])
    blocks = part_recv[0]
    for block in range(1, EV):
        blocks = blocks + part_recv[block]
    blocks = blocks * NEV ** (-1.5)
    line, entry = iota((32, NEV), 0), iota((32, NEV), 1)
    lines = jnp.concatenate(
        [jnp.broadcast_to(blocks[part : part + 1], (16, NEV)) for part in range(2)], 0
    )
    lines = jnp.where(line % 16 == entry // NS, lines, 0.0)
    picked = iota((NEV, NS), 0) % NS == iota((NEV, NS), 1)
    final = lax.dot_general(
        three_parts(lines), jnp.where(picked, 1.0, 0.0).astype(BF16), NN,
        preferred_element_type=F32,
    ).reshape(3, 32, NS)
    blocks_ref[...] = (final[0] + (final[1] + final[2])).reshape(blocks_ref.shape)
    padded = jnp.concatenate([blocks, jnp.zeros((14, NEV), F32)], 0)
    met = lax.dot_general(
        three_parts(padded), counts[...], NN, preferred_element_type=F32
    ).reshape(3, 16, 2 * NEV)
    met = met[0] + (met[1] + met[2])
    met = met[:, :NEV] + met[:, NEV:]
    real_value = met[0:1] * blocks[0:1] - met[1:2] * blocks[1:2]
    imag_value = met[0:1] * blocks[1:2] + met[1:2] * blocks[0:1]
    value = [part.sum(axis=1, keepdims=True) for part in (real_value, imag_value)]
    corr_ref[...] = jnp.concatenate(value, 1) / math.sqrt(DIAG_T)

    arrived(part_recv.at[others], part_sem.at[0])


def place(blocks_in, corr_in, blocks_ref, corr_ref):
    blocks_ref[...] = blocks_in[...]
    corr_ref[...] = corr_in[...]


def shards(
    sink_elemental,
    source_elemental,
    perambulator,
    diagram_time,
    diagram_perm,
    diagram_ops,
    diagram_sign,
):
    source = jnp.transpose(source_elemental, (0, 1, 3, 4, 2)).reshape(2, NS, ROWS, NEV)
    count = diagram_time.shape[0]
    whole = pl.BlockSpec(memory_space=pl.ANY)
    near = pl.BlockSpec(memory_space=pltpu.VMEM)
    dma = pltpu.SemaphoreType.DMA
    blocks, correlator = pl.pallas_call(
        kernel,
        out_shape=(
            jax.ShapeDtypeStruct((2, 1, 2, NS, NS), F32),
            jax.ShapeDtypeStruct((1, 2), F32),
        ),
        in_specs=[whole] * 7,
        out_specs=(near, near),
        scratch_shapes=[
            pltpu.VMEM(perambulator.shape, BF16),
            pltpu.VMEM((1, count), jnp.int32),
            pltpu.VMEM((2, count), jnp.int32),
            pltpu.VMEM((4, count), jnp.int32),
            pltpu.VMEM((1, count), jnp.int32),
            pltpu.VMEM((BLOCK, 2, NS, NEV, NEV), BF16),
            pltpu.VMEM((EV, BLOCK, ROWS, NEV), jnp.int32),
            pltpu.VMEM((BLOCK, EV, ROWS, NEV), jnp.int32),
            pltpu.VMEM((TM, 2, NS, ROWS, NEV), BF16),
            pltpu.VMEM((BLOCK, 512, EV * NEV), BF16),
            pltpu.VMEM((2 * BLOCK * 2 * NEV, NEV), F32),
            pltpu.VMEM((256, EV * NEV), BF16),
            pltpu.VMEM((512, 256), F32),
            pltpu.VMEM((EV, BLOCK, 1, NEV), F32),
            pltpu.VMEM((BLOCK, EV, 1, NEV), F32),
            pltpu.VMEM((NS * NEV, 2 * NEV), F32),
            pltpu.VMEM((256, 256), BF16),
            pltpu.VMEM((512, 256), BF16),
            pltpu.VMEM((256, 256), BF16),
            pltpu.VMEM((NEV, 2 * NEV), BF16),
            pltpu.VMEM((256, 256), BF16),
            pltpu.VMEM((2, NEV), F32),
            pltpu.VMEM((EV, 2, NEV), F32),
            dma((BLOCK,)),
            dma((BLOCK,)),
            dma((BLOCK,)),
            dma((BLOCK,)),
            dma((2, BLOCK)),
            dma((2,)),
            dma((2, 2, RINGS)),
            dma((2, 2, RINGS)),
            dma((2,)),
            dma,
            dma((5,)),
        ],
        compiler_params=pltpu.CompilerParams(
            collective_id=0, has_side_effects=True, vmem_limit_bytes=60 << 20
        ),
        cost_estimate=pl.CostEstimate(
            flops=17 * 10**9, bytes_accessed=5 << 20, transcendentals=0
        ),
    )(
        sink_elemental,
        source,
        perambulator,
        diagram_time.reshape(1, count),
        diagram_perm.T,
        diagram_ops.T,
        diagram_sign.reshape(1, count),
    )
    blocks, correlator = pl.pallas_call(
        place,
        out_shape=(
            jax.ShapeDtypeStruct(blocks.shape, F32),
            jax.ShapeDtypeStruct(correlator.shape, F32),
        ),
        in_specs=[near, near],
        out_specs=(near, near),
    )(blocks, correlator)
    return blocks, correlator.T


def solution(mesh):
    placed = (
        P(None, "tm", None, "evec", None, None),
        P(None, None, None, "evec", "tm"),
        P(None, "tm", None, None),
        P(),
        P(),
        P(),
        P(),
    )
    return jax.shard_map(
        shards,
        mesh=mesh,
        in_specs=placed,
        out_specs=(P(None, "tm", None, None, None), P(None, "tm")),
        check_vma=False,
    )
```

```python
import functools
import math

import jax
import jax.numpy as jnp
from jax import lax
from jax.experimental import pallas as pl
from jax.experimental.pallas import tpu as pltpu
from jax.sharding import PartitionSpec as P

DIAG_T = 64
NEV = 128
NS = 8
BLOCK = 8
EV = 16
TM = 16
ZS = 8
ROWS = NS * BLOCK
RINGS = 7
TOP = 32767.0
MESH = pl.DeviceIdType.MESH
F32 = jnp.float32
BF16 = jnp.bfloat16
NT = (((1,), (1,)), ((), ()))
NN = (((1,), (0,)), ((), ()))
FAR_FIRST = (10, 9, 11, 6, 14, 2, 8, 5, 7, 13, 15, 1, 3, 4, 12)


def split_parts(value):
    high = value.astype(BF16)
    return high, (value - high.astype(F32)).astype(BF16)


def three_parts(value):
    high = value.astype(BF16)
    middle, low = split_parts(value - high.astype(F32))
    return jnp.concatenate([high, middle, low], 0)


def iota(shape, axis):
    return lax.broadcasted_iota(jnp.int32, shape, axis)


def kernel(
    sink_ref,
    source_ref,
    peram_in,
    time_in,
    perm_in,
    ops_in,
    sign_in,
    blocks_ref,
    corr_ref,
    peram_ref,
    time_ref,
    perm_ref,
    ops_ref,
    sign_ref,
    sink_buf,
    send,
    recv,
    gathered,
    rmat,
    stage,
    tmat,
    total,
    scale_own,
    scale_recv,
    wide,
    left_mat,
    right_mat,
    source_mat,
    counts,
    spread,
    part_own,
    part_recv,
    sink_sem,
    send_sem,
    recv_sem,
    own_sem,
    scale_sem,
    part_sem,
    ring_sem,
    pair_sem,
    first_sem,
    slot_sem,
    small_sem,
):
    tm = lax.axis_index("tm")
    ev = lax.axis_index("evec")
    row, column = ev // 4, lax.rem(ev, 4)
    depth, core = tm // 2, lax.rem(tm, 2)

    def peer(step):
        return lax.rem(row + step // 4, 4) * 4 + lax.rem(column + step % 4, 4)

    def slot(step):
        return lax.rem(depth + step + ZS, ZS) * 2 + core

    up, down = (slot(1), ev), (slot(-1), ev)
    pair = (depth * 2 + 1 - core, ev)

    def sink_copy(a):
        return pltpu.make_async_copy(
            sink_ref.at[:, 0, :, a], sink_buf.at[a], sink_sem.at[a]
        )

    small = [
        pltpu.make_async_copy(whole, near, small_sem.at[at])
        for at, (whole, near) in enumerate(
            (
                (peram_in, peram_ref),
                (time_in, time_ref),
                (perm_in, perm_ref),
                (ops_in, ops_ref),
                (sign_in, sign_ref),
            )
        )
    ]
    small[0].start()
    sink_copy(0).start()
    barrier = pltpu.get_barrier_semaphore()
    for step in FAR_FIRST:
        pl.semaphore_signal(barrier, inc=1, device_id=(tm, peer(step)), device_id_type=MESH)
    for device in (up, down, pair):
        pl.semaphore_signal(barrier, inc=1, device_id=device, device_id_type=MESH)
    for a in range(1, BLOCK):
        sink_copy(a).start()
    small[0].wait()

    real, imag = peram_ref[0, 0], peram_ref[1, 0]
    real32, imag32 = real.astype(F32), imag.astype(F32)
    real_t, imag_t = real32.T.astype(BF16), imag32.T.astype(BF16)
    minus, minus_t = (-imag32).astype(BF16), (-imag32.T).astype(BF16)
    left_mat[...] = jnp.concatenate(
        [jnp.concatenate([real_t, minus_t], 1), jnp.concatenate([imag_t, real_t], 1)], 0
    )
    one = jnp.concatenate(
        [jnp.concatenate([real, imag], 1), jnp.concatenate([minus, real], 1)], 0
    )
    right_mat[...] = jnp.concatenate([one, one], 0)
    source_mat[...] = jnp.concatenate(
        [jnp.concatenate([real, minus], 1), jnp.concatenate([imag, real], 1)], 0
    )

    def transform(a):
        for s2 in range(NS // 2):
            s = 2 * s2
            both = jnp.concatenate(
                [
                    jnp.concatenate([sink_buf[a, 0, s], sink_buf[a, 0, s + 1]], 1),
                    jnp.concatenate([sink_buf[a, 1, s], sink_buf[a, 1, s + 1]], 1),
                ],
                0,
            )
            once = lax.dot_general(left_mat[...], both, NN, preferred_element_type=F32)
            high, low = split_parts(once)
            lines = []
            for h in range(2):
                lanes = slice(h * NEV, (h + 1) * NEV)
                lines.append(
                    jnp.concatenate(
                        [high[:NEV, lanes], high[NEV:, lanes], low[:NEV, lanes], low[NEV:, lanes]], 1
                    )
                )
            wide[pl.ds(s * NEV, 2 * NEV), :] = lax.dot_general(
                jnp.concatenate(lines, 0), right_mat[...], NN, preferred_element_type=F32
            )
    def encode(a, there):
        value = jnp.concatenate(
            [
                wide[pl.ds(pl.multiple_of(s * NEV + there * BLOCK, BLOCK), BLOCK), :]
                for s in range(NS)
            ],
            0,
        )
        top = jnp.max(jnp.abs(value), axis=0, keepdims=True)
        top = jnp.maximum(jnp.maximum(top[:, :NEV], top[:, NEV:]), 1e-35)
        factor = TOP / top
        real_code = jnp.round(value[:, :NEV] * factor).astype(jnp.int32)
        imag_code = jnp.round(value[:, NEV:] * factor).astype(jnp.int32)
        send[there, a] = (real_code << 16) | (imag_code & 0xFFFF)
        scale_own[there, a] = top * (1.0 / TOP)

    def send_copy(a, step):
        there = peer(step)
        return pltpu.make_async_remote_copy(
            send.at[there, a], recv.at[a, ev], send_sem.at[a], recv_sem.at[a],
            device_id=(tm, there), device_id_type=MESH,
        )

    def scale_copy(a, step):
        there = peer(step)
        return pltpu.make_async_remote_copy(
            scale_own.at[there, a], scale_recv.at[a, ev], scale_sem.at[0, a], scale_sem.at[1, a],
            device_id=(tm, there), device_id_type=MESH,
        )

    def own_copy(a):
        return pltpu.make_async_copy(send.at[ev, a], recv.at[a, ev], own_sem.at[a])

    def post(a):
        for step in FAR_FIRST:
            encode(a, peer(step))
            scale_copy(a, step).start()
            send_copy(a, step).start()
        encode(a, ev)
        own_copy(a).start()
        scale_recv[a, ev] = scale_own[ev, a]

    def arrived(ref, sem):
        pltpu.make_async_copy(ref, ref, sem).wait()

    def ring_copy(way, message):
        step, half = message // 2, lax.rem(message + way, 2)
        index = slot(step * (2 * way - 1))
        src = source_ref.at[half] if isinstance(message, int) else gathered.at[index, half]
        return pltpu.make_async_remote_copy(
            src, gathered.at[index, half], ring_sem.at[0, way, message],
            ring_sem.at[1, way, message], device_id=(up, down)[way], device_id_type=MESH,
        )

    def ring_arrival(way, message):
        index = slot((message // 2 + 1) * (2 * way - 1))
        return gathered.at[index, lax.rem(message + way, 2)]

    def pair_copy(way, message):
        ref = ring_arrival(way, message)
        return pltpu.make_async_remote_copy(
            ref, ref, pair_sem.at[0, way, message], pair_sem.at[1, way, message],
            device_id=pair, device_id_type=MESH,
        )

    def pair_arrival(way, message):
        index = slot((message // 2 + 1) * (2 * way - 1)) + 1 - 2 * core
        return gathered.at[index, lax.rem(message + way, 2)]

    pair_first = pltpu.make_async_remote_copy(
        source_ref, gathered.at[tm], first_sem.at[0], first_sem.at[1],
        device_id=pair, device_id_type=MESH,
    )
    own_source = pltpu.make_async_copy(source_ref, gathered.at[tm], slot_sem)

    def relay(message):
        for way in range(2):
            arrived(ring_arrival(way, message), ring_sem.at[1, way, message])
            pair_copy(way, message).start()

        @pl.when(message < 4)
        def _():
            for way in range(2):
                ring_copy(way, message + 2).start()

        @pl.when(message == 4)
        def _():
            ring_copy(0, message + 2).start()

        @pl.when(message == 5)
        def _():
            ring_copy(1, message + 1).start()

    sink_copy(0).wait()
    transform(0)
    pl.semaphore_wait(barrier, EV - 1 + 3)
    for message in range(2):
        for way in range(2):
            ring_copy(way, message).start()
    pair_first.start()
    own_source.start()
    post(0)

    for copy in small[1:]:
        copy.start()

    @pl.loop(1, BLOCK)
    def _(a):
        sink_copy(a).wait()
        transform(a)
        post(a)
        relay(a - 1)

    def position(first):
        nucleon = first // 2
        return (
            perm_ref[nucleon : nucleon + 1, :] * NS + ops_ref[first : first + 1, :]
        ) * NS + ops_ref[first + 1 : first + 2, :]

    for copy in small[1:]:
        copy.wait()
    phase = jnp.where(time_ref[...] == tm, 1 - 2 * sign_ref[...], 0).astype(F32)
    entries = iota((NEV, phase.shape[1]), 0)
    first_hot = jnp.where(entries == position(0), phase, 0.0).astype(BF16)
    second_hot = jnp.where(entries == position(2), 1.0, 0.0).astype(BF16)
    counts[...] = jnp.concatenate(
        split_parts(
            lax.dot_general(first_hot, second_hot, NT, preferred_element_type=F32)
        ),
        1,
    )

    own_source.wait()
    arrived(gathered.at[tm + 1 - 2 * core], first_sem.at[1])

    @pl.loop(0, RINGS)
    def _(message):
        for way in range(2):
            arrived(pair_arrival(way, message), pair_sem.at[1, way, message])

    @pl.loop(0, NS)
    def _(u):
        for j2 in range(BLOCK // 2):
            mats = []
            for part in range(2):
                lines = gathered[:, part, u, pl.ds(j2 * 2 * BLOCK, 2 * BLOCK), :].astype(F32)
                mats.append(
                    [
                        lines[:, h * BLOCK : (h + 1) * BLOCK].reshape(NEV, NEV).astype(BF16)
                        for h in range(2)
                    ]
                )
            by_rows = jnp.concatenate(
                [jnp.concatenate([mats[0][h], mats[1][h]], 1) for h in range(2)], 0
            )
            by_lanes = jnp.concatenate(
                [jnp.concatenate([mats[part][0], mats[part][1]], 1) for part in range(2)], 0
            )
            direct = lax.dot_general(source_mat[...], by_rows, NT, preferred_element_type=F32)
            crossed = lax.dot_general(source_mat[...], by_lanes, NN, preferred_element_type=F32)
            for p, result in enumerate((direct, crossed)):
                for h in range(2):
                    at = (p * BLOCK + 2 * j2 + h) * 2 * NEV
                    stage[pl.ds(at, 2 * NEV), :] = result[:, h * NEV : (h + 1) * NEV]

        @pl.loop(0, EV)
        def _(block):
            lanes = pl.ds(pl.multiple_of(block * NEV, NEV), NEV)
            for p in range(2):
                turned = []
                for part in range(2):
                    tiles = [
                        stage[
                            pl.ds((p * BLOCK + j) * 2 * NEV + part * NEV + block * BLOCK, BLOCK), :
                        ]
                        for j in range(BLOCK)
                    ]
                    turned.append(jnp.swapaxes(jnp.stack(tiles, 0), 0, 1))
                rows = pl.ds(pl.multiple_of((p * NS + u) * 32, 32), 32)
                for a in range(BLOCK):
                    parts = []
                    for part in range(2):
                        value = turned[part][a]
                        parts += [value, value - value.astype(BF16).astype(F32)]
                    rmat[a, rows, lanes] = jnp.concatenate(parts, 0).astype(BF16)

    total[...] = jnp.zeros_like(total)
    tile_row, entry = iota((256, 256), 0), iota((256, 256), 1)
    spread[...] = jnp.where(
        (tile_row // 128 == entry // 128) & (tile_row // BLOCK % NS == entry // NS % NS), 1.0, 0.0
    ).astype(BF16)

    others = pl.ds(0, EV - 1)
    pair_first.wait_send()

    @pl.loop(0, RINGS)
    def _(message):
        for way in range(2):
            arrived(pair_arrival(way, message), ring_sem.at[0, way, message])
            arrived(pair_arrival(way, message), pair_sem.at[0, way, message])

    @pl.loop(0, BLOCK)
    def _(a):
        own_copy(a).wait()
        arrived(scale_recv.at[a, others], scale_sem.at[0, a])
        arrived(recv.at[a, others], send_sem.at[a])
        arrived(scale_recv.at[a, others], scale_sem.at[1, a])
        arrived(recv.at[a, others], recv_sem.at[a])
        for block in range(EV):
            scale = scale_recv[a, block]
            packed = recv[a, block]
            real_high, real_low = split_parts((packed >> 16).astype(F32) * scale)
            imag_high, imag_low = split_parts(((packed << 16) >> 16).astype(F32) * scale)
            tmat[:, block * NEV : (block + 1) * NEV] = jnp.concatenate(
                [real_high, real_low, imag_high, imag_low], 0
            )
        total[...] += lax.dot_general(rmat[a], tmat[...], NT, preferred_element_type=F32)

    alike = (iota((512, 256), 0) % BLOCK) == (iota((512, 256), 1) % BLOCK)
    kept = jnp.where(alike, total[...], 0.0).reshape(32, 16, 256).sum(axis=1)
    lined = lax.dot_general(
        three_parts(kept), spread[...], NN, preferred_element_type=F32
    ).reshape(3, 32, 256)
    lined = lined[0] + (lined[1] + lined[2])
    line, entry = iota((32, 128), 0), iota((32, 128), 1)
    wanted = (line // 16 == entry // 64) & (line // 2 % NS == entry % NS)
    real_line = line % 2 == 0
    with_real, with_imag = lined[:, :NEV], lined[:, NEV:]
    real_sum = jnp.where(wanted, jnp.where(real_line, with_real, -with_imag), 0.0)
    imag_sum = jnp.where(wanted, jnp.where(real_line, with_imag, with_real), 0.0)
    part_own[...] = jnp.concatenate(
        [real_sum.sum(axis=0, keepdims=True), imag_sum.sum(axis=0, keepdims=True)], 0
    )

    def part_copy(step):
        return pltpu.make_async_remote_copy(
            part_own, part_recv.at[ev], part_sem.at[0], part_sem.at[1],
            device_id=(tm, peer(step)), device_id_type=MESH,
        )

    for step in FAR_FIRST:
        part_copy(step).start()
    part_recv[ev] = part_own[...]
    arrived(part_recv.at[others], part_sem.at[1])
    blocks = part_recv[0]
    for block in range(1, EV):
        blocks = blocks + part_recv[block]
    blocks = blocks * NEV ** (-1.5)
    line, entry = iota((32, NEV), 0), iota((32, NEV), 1)
    lines = jnp.concatenate(
        [jnp.broadcast_to(blocks[part : part + 1], (16, NEV)) for part in range(2)], 0
    )
    lines = jnp.where(line % 16 == entry // NS, lines, 0.0)
    picked = iota((NEV, NS), 0) % NS == iota((NEV, NS), 1)
    final = lax.dot_general(
        three_parts(lines), jnp.where(picked, 1.0, 0.0).astype(BF16), NN,
        preferred_element_type=F32,
    ).reshape(3, 32, NS)
    blocks_ref[...] = (final[0] + (final[1] + final[2])).reshape(blocks_ref.shape)
    padded = jnp.concatenate([blocks, jnp.zeros((14, NEV), F32)], 0)
    met = lax.dot_general(
        three_parts(padded), counts[...], NN, preferred_element_type=F32
    ).reshape(3, 16, 2 * NEV)
    met = met[0] + (met[1] + met[2])
    met = met[:, :NEV] + met[:, NEV:]
    real_value = met[0:1] * blocks[0:1] - met[1:2] * blocks[1:2]
    imag_value = met[0:1] * blocks[1:2] + met[1:2] * blocks[0:1]
    value = [part.sum(axis=1, keepdims=True) for part in (real_value, imag_value)]
    corr_ref[...] = jnp.concatenate(value, 1) / math.sqrt(DIAG_T)

    arrived(part_recv.at[others], part_sem.at[0])


def place(blocks_in, corr_in, blocks_ref, corr_ref):
    blocks_ref[...] = blocks_in[...]
    corr_ref[...] = corr_in[...]


def shards(
    sink_elemental,
    source_elemental,
    perambulator,
    diagram_time,
    diagram_perm,
    diagram_ops,
    diagram_sign,
):
    source = jnp.transpose(source_elemental, (0, 1, 3, 4, 2)).reshape(2, NS, ROWS, NEV)
    count = diagram_time.shape[0]
    whole = pl.BlockSpec(memory_space=pl.ANY)
    near = pl.BlockSpec(memory_space=pltpu.VMEM)
    dma = pltpu.SemaphoreType.DMA
    blocks, correlator = pl.pallas_call(
        kernel,
        out_shape=(
            jax.ShapeDtypeStruct((2, 1, 2, NS, NS), F32),
            jax.ShapeDtypeStruct((1, 2), F32),
        ),
        in_specs=[whole] * 7,
        out_specs=(near, near),
        scratch_shapes=[
            pltpu.VMEM(perambulator.shape, BF16),
            pltpu.VMEM((1, count), jnp.int32),
            pltpu.VMEM((2, count), jnp.int32),
            pltpu.VMEM((4, count), jnp.int32),
            pltpu.VMEM((1, count), jnp.int32),
            pltpu.VMEM((BLOCK, 2, NS, NEV, NEV), BF16),
            pltpu.VMEM((EV, BLOCK, ROWS, NEV), jnp.int32),
            pltpu.VMEM((BLOCK, EV, ROWS, NEV), jnp.int32),
            pltpu.VMEM((TM, 2, NS, ROWS, NEV), BF16),
            pltpu.VMEM((BLOCK, 512, EV * NEV), BF16),
            pltpu.VMEM((2 * BLOCK * 2 * NEV, NEV), F32),
            pltpu.VMEM((256, EV * NEV), BF16),
            pltpu.VMEM((512, 256), F32),
            pltpu.VMEM((EV, BLOCK, 1, NEV), F32),
            pltpu.VMEM((BLOCK, EV, 1, NEV), F32),
            pltpu.VMEM((NS * NEV, 2 * NEV), F32),
            pltpu.VMEM((256, 256), BF16),
            pltpu.VMEM((512, 256), BF16),
            pltpu.VMEM((256, 256), BF16),
            pltpu.VMEM((NEV, 2 * NEV), BF16),
            pltpu.VMEM((256, 256), BF16),
            pltpu.VMEM((2, NEV), F32),
            pltpu.VMEM((EV, 2, NEV), F32),
            dma((BLOCK,)),
            dma((BLOCK,)),
            dma((BLOCK,)),
            dma((BLOCK,)),
            dma((2, BLOCK)),
            dma((2,)),
            dma((2, 2, RINGS)),
            dma((2, 2, RINGS)),
            dma((2,)),
            dma,
            dma((5,)),
        ],
        compiler_params=pltpu.CompilerParams(
            collective_id=0, has_side_effects=True, vmem_limit_bytes=60 << 20
        ),
        cost_estimate=pl.CostEstimate(
            flops=17 * 10**9, bytes_accessed=5 << 20, transcendentals=0
        ),
    )(
        sink_elemental,
        source,
        perambulator,
        diagram_time.reshape(1, count),
        diagram_perm.T,
        diagram_ops.T,
        diagram_sign.reshape(1, count),
    )
    blocks, correlator = pl.pallas_call(
        place,
        out_shape=(
            jax.ShapeDtypeStruct(blocks.shape, F32),
            jax.ShapeDtypeStruct(correlator.shape, F32),
        ),
        in_specs=[near, near],
        out_specs=(near, near),
    )(blocks, correlator)
    return blocks, correlator.T


def solution(mesh):
    placed = (
        P(None, "tm", None, "evec", None, None),
        P(None, None, None, "evec", "tm"),
        P(None, "tm", None, None),
        P(),
        P(),
        P(),
        P(),
    )
    return jax.shard_map(
        shards,
        mesh=mesh,
        in_specs=placed,
        out_specs=(P(None, "tm", None, None, None), P(None, "tm")),
        check_vma=False,
    )
```

```python
import functools
import math

import jax
import jax.numpy as jnp
from jax import lax
from jax.experimental import pallas as pl
from jax.experimental.pallas import tpu as pltpu
from jax.sharding import PartitionSpec as P

DIAG_T = 64
NEV = 128
NS = 8
BLOCK = 8
EV = 16
TM = 16
ZS = 8
ROWS = NS * BLOCK
RINGS = 7
TOP = 32767.0
MESH = pl.DeviceIdType.MESH
F32 = jnp.float32
BF16 = jnp.bfloat16
NT = (((1,), (1,)), ((), ()))
NN = (((1,), (0,)), ((), ()))
FAR_FIRST = (10, 9, 11, 6, 14, 2, 8, 5, 7, 13, 15, 1, 3, 4, 12)


def split_parts(value):
    high = value.astype(BF16)
    return high, (value - high.astype(F32)).astype(BF16)


def three_parts(value):
    high = value.astype(BF16)
    middle, low = split_parts(value - high.astype(F32))
    return jnp.concatenate([high, middle, low], 0)


def iota(shape, axis):
    return lax.broadcasted_iota(jnp.int32, shape, axis)


def kernel(
    sink_ref,
    source_ref,
    peram_in,
    time_in,
    perm_in,
    ops_in,
    sign_in,
    blocks_ref,
    corr_ref,
    peram_ref,
    time_ref,
    perm_ref,
    ops_ref,
    sign_ref,
    sink_buf,
    send,
    recv,
    gathered,
    rmat,
    stage,
    tmat,
    total,
    scale_own,
    scale_recv,
    wide,
    left_mat,
    right_mat,
    source_mat,
    counts,
    spread,
    part_own,
    part_recv,
    sink_sem,
    send_sem,
    recv_sem,
    own_sem,
    scale_sem,
    part_sem,
    ring_sem,
    pair_sem,
    first_sem,
    slot_sem,
    small_sem,
):
    tm = lax.axis_index("tm")
    ev = lax.axis_index("evec")
    row, column = ev // 4, lax.rem(ev, 4)
    depth, core = tm // 2, lax.rem(tm, 2)

    def peer(step):
        return lax.rem(row + step // 4, 4) * 4 + lax.rem(column + step % 4, 4)

    def slot(step):
        return lax.rem(depth + step + ZS, ZS) * 2 + core

    up, down = (slot(1), ev), (slot(-1), ev)
    pair = (depth * 2 + 1 - core, ev)

    def sink_copy(a):
        return pltpu.make_async_copy(
            sink_ref.at[:, 0, :, a], sink_buf.at[a], sink_sem.at[a]
        )

    small = [
        pltpu.make_async_copy(whole, near, small_sem.at[at])
        for at, (whole, near) in enumerate(
            (
                (peram_in, peram_ref),
                (time_in, time_ref),
                (perm_in, perm_ref),
                (ops_in, ops_ref),
                (sign_in, sign_ref),
            )
        )
    ]
    small[0].start()
    sink_copy(0).start()
    barrier = pltpu.get_barrier_semaphore()
    for step in FAR_FIRST:
        pl.semaphore_signal(barrier, inc=1, device_id=(tm, peer(step)), device_id_type=MESH)
    for device in (up, down, pair):
        pl.semaphore_signal(barrier, inc=1, device_id=device, device_id_type=MESH)
    for a in range(1, BLOCK):
        sink_copy(a).start()
    small[0].wait()

    real, imag = peram_ref[0, 0], peram_ref[1, 0]
    real32, imag32 = real.astype(F32), imag.astype(F32)
    real_t, imag_t = real32.T.astype(BF16), imag32.T.astype(BF16)
    minus, minus_t = (-imag32).astype(BF16), (-imag32.T).astype(BF16)
    left_mat[...] = jnp.concatenate(
        [jnp.concatenate([real_t, minus_t], 1), jnp.concatenate([imag_t, real_t], 1)], 0
    )
    one = jnp.concatenate(
        [jnp.concatenate([real, imag], 1), jnp.concatenate([minus, real], 1)], 0
    )
    right_mat[...] = jnp.concatenate([one, one], 0)
    source_mat[...] = jnp.concatenate(
        [jnp.concatenate([real, minus], 1), jnp.concatenate([imag, real], 1)], 0
    )

    def transform(a):
        for s2 in range(NS // 2):
            s = 2 * s2
            both = jnp.concatenate(
                [
                    jnp.concatenate([sink_buf[a, 0, s], sink_buf[a, 0, s + 1]], 1),
                    jnp.concatenate([sink_buf[a, 1, s], sink_buf[a, 1, s + 1]], 1),
                ],
                0,
            )
            once = lax.dot_general(left_mat[...], both, NN, preferred_element_type=F32)
            high, low = split_parts(once)
            lines = []
            for h in range(2):
                lanes = slice(h * NEV, (h + 1) * NEV)
                lines.append(
                    jnp.concatenate(
                        [high[:NEV, lanes], high[NEV:, lanes], low[:NEV, lanes], low[NEV:, lanes]], 1
                    )
                )
            wide[pl.ds(s * NEV, 2 * NEV), :] = lax.dot_general(
                jnp.concatenate(lines, 0), right_mat[...], NN, preferred_element_type=F32
            )
    def encode(a, there):
        value = jnp.concatenate(
            [
                wide[pl.ds(pl.multiple_of(s * NEV + there * BLOCK, BLOCK), BLOCK), :]
                for s in range(NS)
            ],
            0,
        )
        top = jnp.max(jnp.abs(value), axis=0, keepdims=True)
        top = jnp.maximum(jnp.maximum(top[:, :NEV], top[:, NEV:]), 1e-35)
        factor = TOP / top
        real_code = jnp.round(value[:, :NEV] * factor).astype(jnp.int32)
        imag_code = jnp.round(value[:, NEV:] * factor).astype(jnp.int32)
        send[there, a] = (real_code << 16) | (imag_code & 0xFFFF)
        scale_own[there, a] = top * (1.0 / TOP)

    def send_copy(a, step):
        there = peer(step)
        return pltpu.make_async_remote_copy(
            send.at[there, a], recv.at[a, ev], send_sem.at[a], recv_sem.at[a],
            device_id=(tm, there), device_id_type=MESH,
        )

    def scale_copy(a, step):
        there = peer(step)
        return pltpu.make_async_remote_copy(
            scale_own.at[there, a], scale_recv.at[a, ev], scale_sem.at[0, a], scale_sem.at[1, a],
            device_id=(tm, there), device_id_type=MESH,
        )

    def own_copy(a):
        return pltpu.make_async_copy(send.at[ev, a], recv.at[a, ev], own_sem.at[a])

    def post(a):
        for step in FAR_FIRST:
            encode(a, peer(step))
            scale_copy(a, step).start()
            send_copy(a, step).start()
        encode(a, ev)
        own_copy(a).start()
        scale_recv[a, ev] = scale_own[ev, a]

    def arrived(ref, sem):
        pltpu.make_async_copy(ref, ref, sem).wait()

    def ring_copy(way, message):
        step, half = message // 2, lax.rem(message + way, 2)
        index = slot(step * (2 * way - 1))
        src = source_ref.at[half] if isinstance(message, int) else gathered.at[index, half]
        return pltpu.make_async_remote_copy(
            src, gathered.at[index, half], ring_sem.at[0, way, message],
            ring_sem.at[1, way, message], device_id=(up, down)[way], device_id_type=MESH,
        )

    def ring_arrival(way, message):
        index = slot((message // 2 + 1) * (2 * way - 1))
        return gathered.at[index, lax.rem(message + way, 2)]

    def pair_copy(way, message):
        ref = ring_arrival(way, message)
        return pltpu.make_async_remote_copy(
            ref, ref, pair_sem.at[0, way, message], pair_sem.at[1, way, message],
            device_id=pair, device_id_type=MESH,
        )

    def pair_arrival(way, message):
        index = slot((message // 2 + 1) * (2 * way - 1)) + 1 - 2 * core
        return gathered.at[index, lax.rem(message + way, 2)]

    pair_first = pltpu.make_async_remote_copy(
        source_ref, gathered.at[tm], first_sem.at[0], first_sem.at[1],
        device_id=pair, device_id_type=MESH,
    )
    own_source = pltpu.make_async_copy(source_ref, gathered.at[tm], slot_sem)

    def relay(message):
        for way in range(2):
            arrived(ring_arrival(way, message), ring_sem.at[1, way, message])
            pair_copy(way, message).start()

        @pl.when(message < 4)
        def _():
            for way in range(2):
                ring_copy(way, message + 2).start()

        @pl.when(message == 4)
        def _():
            ring_copy(0, message + 2).start()

        @pl.when(message == 5)
        def _():
            ring_copy(1, message + 1).start()

    sink_copy(0).wait()
    transform(0)
    pl.semaphore_wait(barrier, EV - 1 + 3)
    for message in range(2):
        for way in range(2):
            ring_copy(way, message).start()
    pair_first.start()
    own_source.start()
    post(0)

    for copy in small[1:]:
        copy.start()

    @pl.loop(1, BLOCK)
    def _(a):
        sink_copy(a).wait()
        transform(a)
        post(a)
        relay(a - 1)

    def position(first):
        nucleon = first // 2
        return (
            perm_ref[nucleon : nucleon + 1, :] * NS + ops_ref[first : first + 1, :]
        ) * NS + ops_ref[first + 1 : first + 2, :]

    for copy in small[1:]:
        copy.wait()
    phase = jnp.where(time_ref[...] == tm, 1 - 2 * sign_ref[...], 0).astype(F32)
    entries = iota((NEV, phase.shape[1]), 0)
    first_hot = jnp.where(entries == position(0), phase, 0.0).astype(BF16)
    second_hot = jnp.where(entries == position(2), 1.0, 0.0).astype(BF16)
    counts[...] = jnp.concatenate(
        split_parts(
            lax.dot_general(first_hot, second_hot, NT, preferred_element_type=F32)
        ),
        1,
    )

    own_source.wait()
    arrived(gathered.at[tm + 1 - 2 * core], first_sem.at[1])

    @pl.loop(0, RINGS)
    def _(message):
        for way in range(2):
            arrived(pair_arrival(way, message), pair_sem.at[1, way, message])

    @pl.loop(0, NS)
    def _(u):
        for j2 in range(BLOCK // 2):
            mats = []
            for part in range(2):
                lines = gathered[:, part, u, pl.ds(j2 * 2 * BLOCK, 2 * BLOCK), :].astype(F32)
                mats.append(
                    [
                        lines[:, h * BLOCK : (h + 1) * BLOCK].reshape(NEV, NEV).astype(BF16)
                        for h in range(2)
                    ]
                )
            by_rows = jnp.concatenate(
                [jnp.concatenate([mats[0][h], mats[1][h]], 1) for h in range(2)], 0
            )
            by_lanes = jnp.concatenate(
                [jnp.concatenate([mats[part][0], mats[part][1]], 1) for part in range(2)], 0
            )
            direct = lax.dot_general(source_mat[...], by_rows, NT, preferred_element_type=F32)
            crossed = lax.dot_general(source_mat[...], by_lanes, NN, preferred_element_type=F32)
            for p, result in enumerate((direct, crossed)):
                for h in range(2):
                    at = (p * BLOCK + 2 * j2 + h) * 2 * NEV
                    stage[pl.ds(at, 2 * NEV), :] = result[:, h * NEV : (h + 1) * NEV]

        @pl.loop(0, EV)
        def _(block):
            lanes = pl.ds(pl.multiple_of(block * NEV, NEV), NEV)
            for p in range(2):
                turned = []
                for part in range(2):
                    tiles = [
                        stage[
                            pl.ds((p * BLOCK + j) * 2 * NEV + part * NEV + block * BLOCK, BLOCK), :
                        ]
                        for j in range(BLOCK)
                    ]
                    turned.append(jnp.swapaxes(jnp.stack(tiles, 0), 0, 1))
                rows = pl.ds(pl.multiple_of((p * NS + u) * 32, 32), 32)
                for a in range(BLOCK):
                    parts = []
                    for part in range(2):
                        value = turned[part][a]
                        parts += [value, value - value.astype(BF16).astype(F32)]
                    rmat[a, rows, lanes] = jnp.concatenate(parts, 0).astype(BF16)

    total[...] = jnp.zeros_like(total)
    tile_row, entry = iota((256, 256), 0), iota((256, 256), 1)
    spread[...] = jnp.where(
        (tile_row // 128 == entry // 128) & (tile_row // BLOCK % NS == entry // NS % NS), 1.0, 0.0
    ).astype(BF16)

    others = pl.ds(0, EV - 1)
    pair_first.wait_send()

    @pl.loop(0, RINGS)
    def _(message):
        for way in range(2):
            arrived(pair_arrival(way, message), ring_sem.at[0, way, message])
            arrived(pair_arrival(way, message), pair_sem.at[0, way, message])

    @pl.loop(0, BLOCK)
    def _(a):
        own_copy(a).wait()
        arrived(scale_recv.at[a, others], scale_sem.at[0, a])
        arrived(recv.at[a, others], send_sem.at[a])
        arrived(scale_recv.at[a, others], scale_sem.at[1, a])
        arrived(recv.at[a, others], recv_sem.at[a])
        for block in range(EV):
            scale = scale_recv[a, block]
            packed = recv[a, block]
            real_high, real_low = split_parts((packed >> 16).astype(F32) * scale)
            imag_high, imag_low = split_parts(((packed << 16) >> 16).astype(F32) * scale)
            tmat[:, block * NEV : (block + 1) * NEV] = jnp.concatenate(
                [real_high, real_low, imag_high, imag_low], 0
            )
        total[...] += lax.dot_general(rmat[a], tmat[...], NT, preferred_element_type=F32)

    alike = (iota((512, 256), 0) % BLOCK) == (iota((512, 256), 1) % BLOCK)
    kept = jnp.where(alike, total[...], 0.0).reshape(32, 16, 256).sum(axis=1)
    lined = lax.dot_general(
        three_parts(kept), spread[...], NN, preferred_element_type=F32
    ).reshape(3, 32, 256)
    lined = lined[0] + (lined[1] + lined[2])
    line, entry = iota((32, 128), 0), iota((32, 128), 1)
    wanted = (line // 16 == entry // 64) & (line // 2 % NS == entry % NS)
    real_line = line % 2 == 0
    with_real, with_imag = lined[:, :NEV], lined[:, NEV:]
    real_sum = jnp.where(wanted, jnp.where(real_line, with_real, -with_imag), 0.0)
    imag_sum = jnp.where(wanted, jnp.where(real_line, with_imag, with_real), 0.0)
    part_own[...] = jnp.concatenate(
        [real_sum.sum(axis=0, keepdims=True), imag_sum.sum(axis=0, keepdims=True)], 0
    )

    def part_copy(step):
        return pltpu.make_async_remote_copy(
            part_own, part_recv.at[ev], part_sem.at[0], part_sem.at[1],
            device_id=(tm, peer(step)), device_id_type=MESH,
        )

    for step in FAR_FIRST:
        part_copy(step).start()
    part_recv[ev] = part_own[...]
    arrived(part_recv.at[others], part_sem.at[1])
    blocks = part_recv[0]
    for block in range(1, EV):
        blocks = blocks + part_recv[block]
    blocks = blocks * NEV ** (-1.5)
    line, entry = iota((32, NEV), 0), iota((32, NEV), 1)
    lines = jnp.concatenate(
        [jnp.broadcast_to(blocks[part : part + 1], (16, NEV)) for part in range(2)], 0
    )
    lines = jnp.where(line % 16 == entry // NS, lines, 0.0)
    picked = iota((NEV, NS), 0) % NS == iota((NEV, NS), 1)
    final = lax.dot_general(
        three_parts(lines), jnp.where(picked, 1.0, 0.0).astype(BF16), NN,
        preferred_element_type=F32,
    ).reshape(3, 32, NS)
    blocks_ref[...] = (final[0] + (final[1] + final[2])).reshape(blocks_ref.shape)
    padded = jnp.concatenate([blocks, jnp.zeros((14, NEV), F32)], 0)
    met = lax.dot_general(
        three_parts(padded), counts[...], NN, preferred_element_type=F32
    ).reshape(3, 16, 2 * NEV)
    met = met[0] + (met[1] + met[2])
    met = met[:, :NEV] + met[:, NEV:]
    real_value = met[0:1] * blocks[0:1] - met[1:2] * blocks[1:2]
    imag_value = met[0:1] * blocks[1:2] + met[1:2] * blocks[0:1]
    value = [part.sum(axis=1, keepdims=True) for part in (real_value, imag_value)]
    corr_ref[...] = jnp.concatenate(value, 1) / math.sqrt(DIAG_T)

    arrived(part_recv.at[others], part_sem.at[0])


def shards(
    sink_elemental,
    source_elemental,
    perambulator,
    diagram_time,
    diagram_perm,
    diagram_ops,
    diagram_sign,
):
    source = jnp.transpose(source_elemental, (0, 1, 3, 4, 2)).reshape(2, NS, ROWS, NEV)
    count = diagram_time.shape[0]
    whole = pl.BlockSpec(memory_space=pl.ANY)
    near = pl.BlockSpec(memory_space=pltpu.VMEM)
    dma = pltpu.SemaphoreType.DMA
    blocks, correlator = pl.pallas_call(
        kernel,
        out_shape=(
            pltpu.VMEM((2, 1, 2, NS, NS), F32),
            pltpu.VMEM((1, 2), F32),
        ),
        in_specs=[whole] * 7,
        out_specs=(near, near),
        scratch_shapes=[
            pltpu.VMEM(perambulator.shape, BF16),
            pltpu.VMEM((1, count), jnp.int32),
            pltpu.VMEM((2, count), jnp.int32),
            pltpu.VMEM((4, count), jnp.int32),
            pltpu.VMEM((1, count), jnp.int32),
            pltpu.VMEM((BLOCK, 2, NS, NEV, NEV), BF16),
            pltpu.VMEM((EV, BLOCK, ROWS, NEV), jnp.int32),
            pltpu.VMEM((BLOCK, EV, ROWS, NEV), jnp.int32),
            pltpu.VMEM((TM, 2, NS, ROWS, NEV), BF16),
            pltpu.VMEM((BLOCK, 512, EV * NEV), BF16),
            pltpu.VMEM((2 * BLOCK * 2 * NEV, NEV), F32),
            pltpu.VMEM((256, EV * NEV), BF16),
            pltpu.VMEM((512, 256), F32),
            pltpu.VMEM((EV, BLOCK, 1, NEV), F32),
            pltpu.VMEM((BLOCK, EV, 1, NEV), F32),
            pltpu.VMEM((NS * NEV, 2 * NEV), F32),
            pltpu.VMEM((256, 256), BF16),
            pltpu.VMEM((512, 256), BF16),
            pltpu.VMEM((256, 256), BF16),
            pltpu.VMEM((NEV, 2 * NEV), BF16),
            pltpu.VMEM((256, 256), BF16),
            pltpu.VMEM((2, NEV), F32),
            pltpu.VMEM((EV, 2, NEV), F32),
            dma((BLOCK,)),
            dma((BLOCK,)),
            dma((BLOCK,)),
            dma((BLOCK,)),
            dma((2, BLOCK)),
            dma((2,)),
            dma((2, 2, RINGS)),
            dma((2, 2, RINGS)),
            dma((2,)),
            dma,
            dma((5,)),
        ],
        compiler_params=pltpu.CompilerParams(
            collective_id=0, has_side_effects=True, vmem_limit_bytes=60 << 20
        ),
        cost_estimate=pl.CostEstimate(
            flops=17 * 10**9, bytes_accessed=5 << 20, transcendentals=0
        ),
    )(
        sink_elemental,
        source,
        perambulator,
        diagram_time.reshape(1, count),
        diagram_perm.T,
        diagram_ops.T,
        diagram_sign.reshape(1, count),
    )
    return blocks, correlator.T


def solution(mesh):
    placed = (
        P(None, "tm", None, "evec", None, None),
        P(None, None, None, "evec", "tm"),
        P(None, "tm", None, None),
        P(),
        P(),
        P(),
        P(),
    )
    return jax.shard_map(
        shards,
        mesh=mesh,
        in_specs=placed,
        out_specs=(P(None, "tm", None, None, None), P(None, "tm")),
        check_vma=False,
    )
```
